32 devices in a mesh: gx: 2 (over y), gz: 16 (over z, x, core).
Axes of the slice: x: 2, y: 2, z: 4, core: 2. Of those that a mesh axis runs over, the one named last changes fastest.
Arguments:
- state: float32 [5, 4, 64, 512], P(None, 'gx', 'gz'), may hold values from -21 to 21
- cotangent: float32 [5, 4, 64, 512], P(None, 'gx', 'gz'), may hold values from -6 to 6
- local_inverse: float32 [64, 4, 64, 512], P(None, 'gx', 'gz'), may hold values from -0.25 to 1.7
- wall_tags: int32 [2, 4, 64], P(None, 'gx', 'gz'), may hold values 0 or 1
- w_in: float32 [5, 256], replicated, may hold values from -2.5 to 2.5
- b_in: float32 [256], replicated, may hold values from -3 to 3
- w_mid: bfloat16 [256, 256], replicated, may hold values from -0.375 to 0.375
- b_mid: float32 [256], replicated, may hold values from -3 to 3
- w_out: bfloat16 [256, 5], replicated, may hold values from -1.5 to 1.5
Outputs:
- grad_state: float32 [5, 4, 64, 512], P(None, 'gx', 'gz')
- grad_w_in: float32 [5, 256], replicated
- grad_b_in: float32 [256], replicated
- grad_w_mid: float32 [256, 256], replicated
- grad_b_mid: float32 [256], replicated
- grad_w_out: float32 [256, 5], replicated
The draws below stay inside these ranges and needn't reach their ends.
All inputs are finite; a program needn't handle non-finite values. No bound on the sum of `wall_tags` on one device may be relied on, other than what follows from the above.
Results may differ from the reference program's by a relative error of at most 0.0085.
Values sent between devices are 32-bit elements; how exact they have to be, the bound alone decides.
A program may use at most 64 MiB of HBM per device.

```python
import math
import jax
import jax.numpy as jnp
from jax import lax

C = 5
H = 256
P_SIZE = 64
EY = 8
NXE = 4
NZE = 64


def draw_state(key, part):
    first_key, second_key = jax.random.split(key)
    x_pos = jnp.arange(NXE, dtype=jnp.float32) / max(NXE - 1, 1)
    z_pos = jnp.arange(NZE, dtype=jnp.float32) / max(NZE - 1, 1)
    ramp = (1.0 + 2.0 * x_pos)[:, None, None] * (1.0 + 2.0 * z_pos)[None, :, None]
    rough = jax.random.uniform(second_key, (NXE, NZE, EY), jnp.float32, 0.5, 1.5)
    amplitude = jnp.repeat(ramp * rough, P_SIZE, axis=2)
    values = jax.random.truncated_normal(first_key, -3.0, 3.0, (C, NXE, NZE, EY * P_SIZE), jnp.float32)
    return 0.5 * amplitude[None] * values


def draw_local_inverse(key, part):
    first_key, second_key = jax.random.split(key)
    diagonal = jax.random.uniform(first_key, (NXE, NZE, EY, P_SIZE), jnp.float32, 0.6, 1.4)
    spread = 0.075 * jax.random.truncated_normal(second_key, -3.0, 3.0, (P_SIZE, NXE, NZE, EY * P_SIZE), jnp.float32)
    identity = jnp.eye(P_SIZE, dtype=jnp.float32)[:, None, None, None, :]
    diag_part = (identity * diagonal[None]).reshape(P_SIZE, NXE, NZE, EY * P_SIZE)
    return spread + diag_part


def set_ends(drawn, key, smallest, top_value):
    spot = [jax.random.randint(jax.random.fold_in(key, axis), (), 0, length) for axis, length in enumerate(drawn.shape)]
    main_axis = drawn.shape.index(max(drawn.shape))
    beside = spot[:main_axis] + [(spot[main_axis] + 1) % drawn.shape[main_axis]] + spot[main_axis + 1:]
    return drawn.at[tuple(spot)].set(smallest).at[tuple(beside)].set(top_value)


def shard_levels(own_key, shape, pieces, least, largest):
    factor_of, own = 1.0, jax.random.fold_in(own_key, 6)
    for position, shards_of in pieces:
        steps = jnp.exp(jax.random.uniform(jax.random.fold_in(own, position), (shards_of,), jnp.float32, least / len(pieces), largest / len(pieces)))
        factor_of = factor_of * jnp.repeat(steps, shape[position] // shards_of).reshape([-1 if axis == position else 1 for axis in range(len(shape))])
    return factor_of


def normal_values(stream_key, extent, deviation, most, cuts=(), held_as=jnp.bfloat16):
    values = deviation * jax.random.normal(stream_key, extent, jnp.float32)
    if cuts:
        values = values * shard_levels(stream_key, extent, cuts, -0.22, 0.18)
    return jnp.clip(values, -most, most).astype(held_as)


def setup_inputs(seed: int = 0) -> dict:
    streams_of = jax.random.split(jax.random.key(seed), 10)
    return {
        "state": draw_state(jax.random.fold_in(streams_of[9], 71), 0),
        "cotangent": normal_values(streams_of[1], (C, NXE, NZE, EY * P_SIZE), 1.0, 6.0, ((1, 2), (2, 16)), jnp.float32),
        "local_inverse": draw_local_inverse(jax.random.fold_in(streams_of[9], 71), 0),
        "wall_tags": set_ends((jax.random.randint(streams_of[3], (2, NXE, NZE), 0, 2) < 1).astype(jnp.int32), jax.random.fold_in(streams_of[3], 1), 0, 1),
        "w_in": normal_values(streams_of[4], (C, H), C ** -0.5, 2.5, (), jnp.float32),
        "b_in": normal_values(streams_of[5], (H,), 0.5, 3.0, (), jnp.float32),
        "w_mid": normal_values(streams_of[6], (H, H), H ** -0.5, 0.375),
        "b_mid": normal_values(streams_of[7], (H,), 0.5, 3.0, (), jnp.float32),
        "w_out": normal_values(streams_of[8], (H, C), (H // 16) ** -0.5, 1.5),
    }


KAPPA = 0.5
DT_STEP = 0.5
EPS = 1e-06
precise = lax.Precision.HIGHEST

def silu_slope(pre_act):
    sigmoid_value = jax.nn.sigmoid(pre_act)
    return sigmoid_value * (1.0 + pre_act * (1.0 - sigmoid_value))

def inner_rows(first_op, second_op, precision=None):
    return lax.dot_general(first_op, second_op, (((1,), (1,)), ((), ())), precision=precision, preferred_element_type=jnp.float32)

def inner_first(first_op, second_op, precision=None):
    return lax.dot_general(first_op, second_op, (((0,), (0,)), ((), ())), precision=precision, preferred_element_type=jnp.float32)

def face_terms(blocks_view, lower_nb, upper_nb, face_axis):
    lower_term = 0.5 * (lower_nb - jnp.take(blocks_view, 0, axis=face_axis))
    upper_term = 0.5 * (upper_nb - jnp.take(blocks_view, 3, axis=face_axis))
    zero_face = jnp.zeros_like(lower_term)
    return jnp.stack([lower_term, zero_face, zero_face, upper_term], axis=face_axis)

def coupling(blocks_view, lower_x, upper_x, lower_z, upper_z, wall_tags):
    bottom = (1.0 - 2.0 * wall_tags[0].astype(jnp.float32))[None, :, :, None, None, None]
    top_side = (1.0 - 2.0 * wall_tags[1].astype(jnp.float32))[None, :, :, None, None, None]
    lower_y = jnp.concatenate([bottom * blocks_view[:, :, :, :1, :, 0, :], blocks_view[:, :, :, :-1, :, 3, :]], axis=3)
    upper_y = jnp.concatenate([blocks_view[:, :, :, 1:, :, 0, :], top_side * blocks_view[:, :, :, -1:, :, 3, :]], axis=3)
    return face_terms(blocks_view, lower_x, upper_x, 4) + face_terms(blocks_view, lower_y, upper_y, 5) + face_terms(blocks_view, lower_z, upper_z, 6)

def reference(state, cotangent, local_inverse, wall_tags, w_in, b_in, w_mid, b_mid, w_out):
    line_nodes = EY * P_SIZE
    entry_count = C * NXE * NZE * line_nodes
    inv_norm = lax.rsqrt(jnp.sum(state * state) / entry_count + EPS)
    adjoint = jnp.einsum('nikjm,cikjn->cikjm', local_inverse.reshape(P_SIZE, NXE, NZE, EY, P_SIZE), cotangent.reshape(C, NXE, NZE, EY, P_SIZE), precision=precise)
    blocks_view = adjoint.reshape(C, NXE, NZE, EY, 4, 4, 4)
    lower_x = jnp.roll(blocks_view[:, :, :, :, 3], 1, axis=1)
    upper_x = jnp.roll(blocks_view[:, :, :, :, 0], -1, axis=1)
    lower_z = jnp.roll(blocks_view[..., 3], 1, axis=2)
    upper_z = jnp.roll(blocks_view[..., 0], -1, axis=2)
    coupled = coupling(blocks_view, lower_x, upper_x, lower_z, upper_z, wall_tags).reshape(C, NXE, NZE, line_nodes)
    adjoint_flat = adjoint.reshape(C, NXE, NZE, line_nodes)

    def column(carry, inputs):
        state_block, adjoint_block = inputs
        state_rows = state_block.reshape(C, NZE * line_nodes)
        adjoint_rows = adjoint_block.reshape(C, NZE * line_nodes)
        scaled_rows = inv_norm * state_rows
        pre_first = inner_first(w_in, scaled_rows, precise) + b_in[:, None]
        hidden_one = jax.nn.silu(pre_first).astype(jnp.bfloat16)
        pre_second = inner_first(w_mid, hidden_one) + b_mid[:, None]
        hidden_two = jax.nn.silu(pre_second).astype(jnp.bfloat16)
        out_grad = (DT_STEP * adjoint_rows).astype(jnp.bfloat16)
        grad_out = inner_rows(hidden_two, out_grad)
        back_two = jnp.dot(w_out, out_grad, preferred_element_type=jnp.float32)
        delta_two = (back_two * silu_slope(pre_second)).astype(jnp.bfloat16)
        grad_mid = inner_rows(hidden_one, delta_two)
        grad_bmid = lax.optimization_barrier(jnp.sum(delta_two.astype(jnp.float32), axis=1))
        back_one = jnp.dot(w_mid, delta_two, preferred_element_type=jnp.float32)
        delta_one = back_one * silu_slope(pre_first)
        grad_in = inner_rows(scaled_rows, delta_one, precise)
        grad_bin = lax.optimization_barrier(jnp.sum(delta_one, axis=1))
        back_input = jnp.dot(w_in, delta_one, precision=precise, preferred_element_type=jnp.float32)
        new_carry = (carry[0] + grad_in, carry[1] + grad_bin, carry[2] + grad_mid, carry[3] + grad_bmid, carry[4] + grad_out)
        return (new_carry, back_input)
    start = (jnp.zeros((C, H), jnp.float32), jnp.zeros((H,), jnp.float32), jnp.zeros((H, H), jnp.float32), jnp.zeros((H,), jnp.float32), jnp.zeros((H, C), jnp.float32))
    totals, back_blocks = lax.scan(column, start, (jnp.moveaxis(state, 1, 0), jnp.moveaxis(adjoint_flat, 1, 0)))
    back_input = jnp.moveaxis(back_blocks.reshape(NXE, C, NZE, line_nodes), 0, 1)
    grad_state = adjoint_flat + KAPPA * coupled + inv_norm * back_input
    factor = 4.0 / math.sqrt(NXE * NZE * line_nodes)
    return (grad_state, totals[0] * factor, totals[1] * factor, totals[2] * factor, totals[3] * factor, totals[4] * factor)
```

```python
import functools
import math

import jax
import jax.numpy as jnp
from jax import lax
from jax.experimental import pallas as pl
from jax.experimental.pallas import tpu as pltpu
from jax.sharding import PartitionSpec as P

KAPPA = 0.5
DT_STEP = 0.5
EPS = 1e-06
F32 = jnp.float32
BF16 = jnp.bfloat16
MESH = pl.DeviceIdType.MESH


def nt_dot(first_op, second_op):
    return lax.dot_general(
        first_op, second_op, (((1,), (1,)), ((), ())), preferred_element_type=F32
    )


def nn_dot(first_op, second_op):
    return jnp.dot(first_op, second_op, preferred_element_type=F32)


def rounded(value):
    return value.astype(BF16).astype(F32)


def kernel(
    dims,
    state_ref,
    cot_ref,
    inv_ref,
    tags_ref,
    w_in_ref,
    b_in_ref,
    w_mid_ref,
    b_mid_ref,
    w_out_ref,
    gstate_ref,
    gin_ref,
    gbin_ref,
    gmid_ref,
    gbmid_ref,
    gout_ref,
    state_rows,
    grad_rows,
    adj_rows,
    back_rows,
    low_x,
    up_x,
    low_z,
    up_z,
    x_send,
    x_halo,
    z_send,
    z_halo,
    w_first,
    w_back,
    w_mid_t,
    bias_mid,
    joint,
    totals,
    totals_in,
    totals_out,
    norm_mine,
    norm_all,
    core_send,
    core_recv,
    plane_send,
    plane_all,
    line_send,
    line_all,
    gathered,
    norm_sems,
    halo_send_sems,
    halo_recv_sems,
    core_sems,
    plane_send_sems,
    plane_recv_sems,
    line_send_sems,
    line_recv_sems,
    spread_send_sems,
    spread_recv_sems,
    pair_send_sems,
    pair_recv_sems,
):
    gx, gz = dims
    channels, x_elems, z_elems, line = state_ref.shape
    hidden = w_mid_ref.shape[0]
    columns = x_elems * z_elems
    count = gx * gz
    half = hidden // 2
    n_plane, n_line = gx * 2, gz // 4
    part = hidden // n_plane
    my_x, my_z = lax.axis_index("gx"), lax.axis_index("gz")
    me = my_x * gz + my_z
    core, side, level = my_z % 2, (my_z // 2) % 2, my_z // 4
    my_plane = my_x * 2 + side
    other_core = (my_x, my_z + 1 - 2 * core)

    barrier = pltpu.get_barrier_semaphore()

    def greet(step, carry):
        to = lax.rem(me + step, count)
        pl.semaphore_signal(
            barrier, inc=1, device_id=(to // gz, lax.rem(to, gz)), device_id_type=MESH
        )
        return carry

    lax.fori_loop(1, count, greet, 0)

    squares = state_ref[...] * state_ref[...]
    squares = jnp.sum(jnp.sum(squares, axis=0), axis=0)
    folded = squares[:, :128]
    for start in range(128, line, 128):
        folded = folded + squares[:, start : start + 128]
    norm_mine[...] = jnp.sum(folded, axis=0, keepdims=True)

    pl.semaphore_wait(barrier, count - 1)

    def norm_copy(step):
        to = lax.rem(me + step, count)
        return pltpu.make_async_remote_copy(
            src_ref=norm_mine,
            dst_ref=norm_all.at[step - 1],
            send_sem=norm_sems.at[0],
            recv_sem=norm_sems.at[1],
            device_id=(to // gz, lax.rem(to, gz)),
            device_id_type=MESH,
        )

    def send_norm(step, carry):
        norm_copy(step).start()
        return carry

    lax.fori_loop(1, count, send_norm, 0)

    for c in range(channels):
        for i in range(x_elems):
            low_x[c, i * z_elems : (i + 1) * z_elems, :] = cot_ref[c, i]
    lane = lax.broadcasted_iota(jnp.int32, (columns, 128), 1)
    first_lane = lane & 64
    blocks = line // 128

    def adjoint_step(n, sums):
        spot = first_lane + n
        rows = jnp.concatenate([inv_ref[n, i] for i in range(x_elems)], axis=0)
        out = []
        for c in range(channels):
            for t in range(blocks):
                piece = low_x[c, :, t * 128 : (t + 1) * 128]
                spread = jnp.take_along_axis(piece, spot, axis=1)
                out.append(
                    sums[c * blocks + t] + rows[:, t * 128 : (t + 1) * 128] * spread
                )
        return tuple(out)

    zero_tile = jnp.zeros((columns, 128), F32)
    sums = lax.fori_loop(
        0, inv_ref.shape[0], adjoint_step, (zero_tile,) * (channels * blocks), unroll=4
    )
    for c in range(channels):
        for t in range(blocks):
            adj_rows[c, :, t * 128 : (t + 1) * 128] = sums[c * blocks + t]

    for c in range(channels):
        x_send[0, c] = adj_rows[c, 0:z_elems, :]
        x_send[1, c] = adj_rows[c, columns - z_elems : columns, :]
        for i in range(x_elems):
            z_send[0, c * x_elems + i] = adj_rows[c, i * z_elems : i * z_elems + 1, :]
            z_send[1, c * x_elems + i] = adj_rows[
                c, (i + 1) * z_elems - 1 : (i + 1) * z_elems, :
            ]
    halo_copies = []
    for spot, (src, dst, to) in enumerate(
        (
            (x_send.at[0], x_halo.at[1], (lax.rem(my_x + gx - 1, gx), my_z)),
            (x_send.at[1], x_halo.at[0], (lax.rem(my_x + 1, gx), my_z)),
            (z_send.at[0], z_halo.at[1], (my_x, lax.rem(my_z + gz - 1, gz))),
            (z_send.at[1], z_halo.at[0], (my_x, lax.rem(my_z + 1, gz))),
        )
    ):
        copy = pltpu.make_async_remote_copy(
            src_ref=src,
            dst_ref=dst,
            send_sem=halo_send_sems.at[spot],
            recv_sem=halo_recv_sems.at[spot],
            device_id=to,
            device_id_type=MESH,
        )
        copy.start()
        halo_copies.append(copy)

    for i in range(x_elems):
        for k in range(z_elems):
            row = i * z_elems + k
            state_rows[row] = jnp.ones((8, line), F32)
            grad_rows[row] = jnp.zeros((16, line), F32)
            for c in range(channels):
                state_rows[row, c : c + 1, :] = state_ref[c, i, k : k + 1, :]
                grad_rows[row, c : c + 1, :] = DT_STEP * adj_rows[c, row : row + 1, :]
    w_in = w_in_ref[...]
    w_high = rounded(w_in)
    w_low = rounded(w_in - w_high)
    b_in = b_in_ref[...]
    b_high = rounded(b_in)
    b_next = rounded(b_in - b_high)
    b_last = rounded(b_in - b_high - b_next)
    joint_rows = jnp.concatenate(
        [w_high, b_high, b_next, b_last, w_high, jnp.zeros((8 - channels, hidden), F32)]
        + [w_low, jnp.zeros((16 - channels, hidden), F32)],
        axis=0,
    )
    w_first[...] = joint_rows.T.astype(BF16)
    w_back[...] = jnp.concatenate([joint_rows[8:16], joint_rows[16:24]], axis=0).astype(BF16)
    w_mid_t[...] = w_mid_ref[...].astype(F32).T.astype(BF16)
    bias_mid[...] = jnp.broadcast_to(b_mid_ref[...], (line, hidden)).T[:, :]
    totals[...] = jnp.zeros_like(totals)
    totals_in[...] = jnp.zeros_like(totals_in)
    totals_out[...] = jnp.zeros_like(totals_out)

    whole = norm_all.at[pl.ds(0, count - 1)]
    pltpu.make_async_copy(whole, whole, norm_sems.at[0]).wait()
    pltpu.make_async_copy(whole, whole, norm_sems.at[1]).wait()
    sum_squares = norm_mine[...] + jnp.sum(norm_all[0 : count - 1], axis=0)
    sum_squares = jnp.sum(sum_squares, axis=1, keepdims=True)
    entry_count = channels * columns * line * count
    inv_norm = lax.rsqrt(sum_squares / entry_count + EPS)
    row_index = lax.broadcasted_iota(jnp.int32, (8, line), 0)
    scale = jnp.where(row_index < channels, jnp.broadcast_to(inv_norm, (8, line)), 1.0)

    def column(row, carry):
        scaled = state_rows[row] * scale
        high = rounded(scaled)
        low = scaled - high
        inputs = jnp.concatenate([high, low, high, jnp.zeros_like(high)], axis=0).astype(BF16)
        joint[hidden:, :] = inputs
        pre = nn_dot(w_first[...], inputs)
        gate = 0.5 * jnp.tanh(0.5 * pre) + 0.5
        act = pre * gate
        slope_one = gate + act * (1.0 - gate)
        hidden_one = act.astype(BF16)
        joint[:hidden, :] = hidden_one
        pre = nn_dot(w_mid_t[...], hidden_one) + bias_mid[...]
        gate = 0.5 * jnp.tanh(0.5 * pre) + 0.5
        act = pre * gate
        slope_two = gate + act * (1.0 - gate)
        hidden_two = act.astype(BF16)
        out_grad = grad_rows[row].astype(BF16)
        totals_out[...] += nt_dot(out_grad, hidden_two)
        back_two = nn_dot(w_out_ref[...], out_grad[:channels])
        delta_two = (back_two * slope_two).astype(BF16)
        totals[...] += nt_dot(joint[...], delta_two)
        delta_one = (nn_dot(w_mid_ref[...], delta_two) * slope_one).astype(BF16)
        totals_in[...] += nt_dot(inputs, delta_one)
        back = nn_dot(w_back[...], delta_one)
        back = back[:8] + back[8:]
        for c in range(channels):
            back_rows[c, pl.ds(row, 1), :] = back[c : c + 1, :]
        return carry

    lax.fori_loop(0, columns, column, 0)

    top = lax.broadcasted_iota(jnp.int32, (8, hidden), 0)
    mixed = jnp.where(
        top == channels + 1, totals[hidden : hidden + 8], totals_in[0:8] + totals_in[8:16]
    )
    for h in range(2):
        lanes = slice(h * half, (h + 1) * half)
        core_send[h, 0:hidden, :] = totals[0:hidden, lanes]
        core_send[h, hidden : hidden + 8, :] = mixed[:, lanes]
        core_send[h, hidden + 8 : hidden + 16, :] = totals_out[0:8, lanes]
    core_copy = pltpu.make_async_remote_copy(
        src_ref=core_send.at[1 - core],
        dst_ref=core_recv,
        send_sem=core_sems.at[0],
        recv_sem=core_sems.at[1],
        device_id=other_core,
        device_id_type=MESH,
    )
    core_copy.start()

    for copy in halo_copies:
        copy.wait()
    for c in range(channels):
        low_x[c, 0:z_elems, :] = x_halo[0, c]
        up_x[c, columns - z_elems : columns, :] = x_halo[1, c]
        if x_elems > 1:
            low_x[c, z_elems:columns, :] = adj_rows[c, 0 : columns - z_elems, :]
            up_x[c, 0 : columns - z_elems, :] = adj_rows[c, z_elems:columns, :]
        for i in range(x_elems):
            first, last = i * z_elems, (i + 1) * z_elems
            low_z[c, first : first + 1, :] = z_halo[0, c * x_elems + i]
            up_z[c, last - 1 : last, :] = z_halo[1, c * x_elems + i]
            if z_elems > 1:
                low_z[c, first + 1 : last, :] = adj_rows[c, first : last - 1, :]
                up_z[c, first : last - 1, :] = adj_rows[c, first + 1 : last, :]
    lane = lax.broadcasted_iota(jnp.int32, (columns, line), 1)
    row = lax.broadcasted_iota(jnp.int32, (columns, line), 0)
    spot_a, spot_b, spot_c, spot_j = (lane >> 4) & 3, (lane >> 2) & 3, lane & 3, lane >> 6
    bottom = jnp.zeros((columns, line), F32)
    ceiling = jnp.zeros((columns, line), F32)
    for i in range(x_elems):
        for k in range(z_elems):
            here = row == i * z_elems + k
            bottom = jnp.where(here, -2.0 * tags_ref[0, i, k].astype(F32), bottom)
            ceiling = jnp.where(here, -2.0 * tags_ref[1, i, k].astype(F32), ceiling)
    for c in range(channels):
        own = adj_rows[c]
        low_y = jnp.where(spot_j == 0, bottom * own, pltpu.roll(own, 52, 1) - own)
        up_y = jnp.where(
            spot_j == line // 64 - 1, ceiling * own, pltpu.roll(own, line - 52, 1) - own
        )
        jump = (
            jnp.where(spot_a == 0, pltpu.roll(low_x[c], line - 48, 1) - own, 0.0)
            + jnp.where(spot_a == 3, pltpu.roll(up_x[c], 48, 1) - own, 0.0)
            + jnp.where(spot_b == 0, low_y, 0.0)
            + jnp.where(spot_b == 3, up_y, 0.0)
            + jnp.where(spot_c == 0, pltpu.roll(low_z[c], line - 3, 1) - own, 0.0)
            + jnp.where(spot_c == 3, pltpu.roll(up_z[c], 3, 1) - own, 0.0)
        )
        back_rows[c] = own + 0.5 * KAPPA * jump + inv_norm * back_rows[c]
        for i in range(x_elems):
            gstate_ref[c, i] = back_rows[c, i * z_elems : (i + 1) * z_elems, :]

    core_copy.wait()
    for q in range(n_plane):
        mine = core_send[core, q * part : (q + 1) * part, :]
        plane_send[q, 0:part, :] = mine + core_recv[q * part : (q + 1) * part, :]
        plane_send[q, part:, :] = core_send[core, hidden:, :] + core_recv[hidden:, :]
    plane_copies = []
    for d in range(1, n_plane):
        to = lax.rem(my_plane + d, n_plane)
        copy = pltpu.make_async_remote_copy(
            src_ref=plane_send.at[to],
            dst_ref=plane_all.at[my_plane],
            send_sem=plane_send_sems.at[d],
            recv_sem=plane_recv_sems.at[d],
            device_id=(to // 2, level * 4 + lax.rem(to, 2) * 2 + core),
            device_id_type=MESH,
        )
        copy.start()
        plane_copies.append(copy)
    plane_all[my_plane] = plane_send[my_plane]
    for copy in plane_copies:
        copy.wait()
    line_send[...] = sum((plane_all[q] for q in range(1, n_plane)), plane_all[0])
    line_copies = []
    for d in range(1, n_line):
        to = lax.rem(level + d, n_line)
        copy = pltpu.make_async_remote_copy(
            src_ref=line_send,
            dst_ref=line_all.at[level],
            send_sem=line_send_sems.at[d],
            recv_sem=line_recv_sems.at[d],
            device_id=(my_x, to * 4 + side * 2 + core),
            device_id_type=MESH,
        )
        copy.start()
        line_copies.append(copy)
    line_all[level] = line_send[...]
    for copy in line_copies:
        copy.wait()
    factor = 4.0 / math.sqrt(entry_count // channels)
    result = sum((line_all[r] for r in range(1, n_line)), line_all[0])
    gathered[core, my_plane] = factor * result

    def to_pair(slot, d):
        return pltpu.make_async_remote_copy(
            src_ref=gathered.at[core, slot],
            dst_ref=gathered.at[core, slot],
            send_sem=pair_send_sems.at[d],
            recv_sem=pair_recv_sems.at[d],
            device_id=other_core,
            device_id_type=MESH,
        )

    spread_copies = []
    for d in range(1, n_plane):
        to = lax.rem(my_plane + d, n_plane)
        copy = pltpu.make_async_remote_copy(
            src_ref=gathered.at[core, my_plane],
            dst_ref=gathered.at[core, my_plane],
            send_sem=spread_send_sems.at[d],
            recv_sem=spread_recv_sems.at[d],
            device_id=(to // 2, level * 4 + lax.rem(to, 2) * 2 + core),
            device_id_type=MESH,
        )
        copy.start()
        spread_copies.append(copy)
    pair_copies = [to_pair(my_plane, 0)]
    pair_copies[0].start()
    for d in range(1, n_plane):
        spread_copies[d - 1].wait_recv()
        copy = to_pair(lax.rem(my_plane + n_plane - d, n_plane), d)
        copy.start()
        pair_copies.append(copy)
    for copy in spread_copies:
        copy.wait_send()
    for copy in pair_copies:
        copy.wait()
    for h in range(2):
        lanes = slice(h * half, (h + 1) * half)
        for q in range(n_plane):
            gmid_ref[q * part : (q + 1) * part, lanes] = gathered[h, q, 0:part, :]
        small = gathered[h, 0, part : part + 8, :]
        gin_ref[:, lanes] = small[0:channels]
        gbin_ref[:, lanes] = small[channels : channels + 1]
        gbmid_ref[:, lanes] = small[channels + 1 : channels + 2]
        gout_ref[lanes, :] = gathered[h, 0, part + 8 : part + 16, :].T[:, 0:channels]


def per_device(dims, state, cotangent, local_inverse, wall_tags, w_in, b_in, w_mid, b_mid, w_out):
    gx, gz = dims
    channels, x_elems, z_elems, line = state.shape
    hidden = w_mid.shape[0]
    columns = x_elems * z_elems
    n_plane, n_line = gx * 2, gz // 4
    part = hidden // n_plane
    half = hidden // 2
    vmem = pl.BlockSpec(memory_space=pltpu.VMEM)
    smem = pl.BlockSpec(memory_space=pltpu.SMEM)
    rows = pltpu.VMEM((channels, columns, line), F32)
    dma = pltpu.SemaphoreType.DMA
    out = pl.pallas_call(
        functools.partial(kernel, dims),
        out_shape=(
            jax.ShapeDtypeStruct(state.shape, F32),
            jax.ShapeDtypeStruct((channels, hidden), F32),
            jax.ShapeDtypeStruct((1, hidden), F32),
            jax.ShapeDtypeStruct((hidden, hidden), F32),
            jax.ShapeDtypeStruct((1, hidden), F32),
            jax.ShapeDtypeStruct((hidden, channels), F32),
        ),
        in_specs=[vmem, vmem, vmem, smem] + [vmem] * 5,
        out_specs=(vmem,) * 6,
        scratch_shapes=[
            pltpu.VMEM((columns, 8, line), F32),
            pltpu.VMEM((columns, 16, line), F32),
            rows,
            rows,
            rows,
            rows,
            rows,
            rows,
            pltpu.VMEM((2, channels, z_elems, line), F32),
            pltpu.VMEM((2, channels, z_elems, line), F32),
            pltpu.VMEM((2, channels * x_elems, 1, line), F32),
            pltpu.VMEM((2, channels * x_elems, 1, line), F32),
            pltpu.VMEM((hidden, 32), BF16),
            pltpu.VMEM((16, hidden), BF16),
            pltpu.VMEM((hidden, hidden), BF16),
            pltpu.VMEM((hidden, line), F32),
            pltpu.VMEM((hidden + 32, line), BF16),
            pltpu.VMEM((hidden + 32, hidden), F32),
            pltpu.VMEM((32, hidden), F32),
            pltpu.VMEM((16, hidden), F32),
            pltpu.VMEM((1, 128), F32),
            pltpu.VMEM((gx * gz, 1, 128), F32),
            pltpu.VMEM((2, hidden + 16, half), F32),
            pltpu.VMEM((hidden + 16, half), F32),
            pltpu.VMEM((n_plane, part + 16, half), F32),
            pltpu.VMEM((n_plane, part + 16, half), F32),
            pltpu.VMEM((part + 16, half), F32),
            pltpu.VMEM((n_line, part + 16, half), F32),
            pltpu.VMEM((2, n_plane, part + 16, half), F32),
            dma((2,)),
            dma((4,)),
            dma((4,)),
            dma((2,)),
            dma((n_plane,)),
            dma((n_plane,)),
            dma((n_line,)),
            dma((n_line,)),
            dma((n_plane,)),
            dma((n_plane,)),
            dma((n_plane,)),
            dma((n_plane,)),
        ],
        compiler_params=pltpu.CompilerParams(
            collective_id=0, has_side_effects=True, vmem_limit_bytes=40 * 1024 * 1024
        ),
    )(
        state,
        cotangent,
        local_inverse,
        wall_tags,
        w_in,
        b_in.reshape(1, hidden),
        w_mid,
        b_mid.reshape(1, hidden),
        w_out,
    )
    return out[0], out[1], out[2].reshape(hidden), out[3], out[4].reshape(hidden), out[5]


def solution(mesh):
    placed = (
        P(None, "gx", "gz", None),
        P(None, "gx", "gz", None),
        P(None, "gx", "gz", None),
        P(None, "gx", "gz"),
        P(),
        P(),
        P(),
        P(),
        P(),
    )
    return jax.shard_map(
        functools.partial(per_device, (mesh.shape["gx"], mesh.shape["gz"])),
        mesh=mesh,
        in_specs=placed,
        out_specs=(P(None, "gx", "gz", None), P(), P(), P(), P(), P()),
        check_vma=False,
    )
```

```python
import functools
import math

import jax
import jax.numpy as jnp
from jax import lax
from jax.experimental import pallas as pl
from jax.experimental.pallas import tpu as pltpu
from jax.sharding import PartitionSpec as P

KAPPA = 0.5
DT_STEP = 0.5
EPS = 1e-06
F32 = jnp.float32
BF16 = jnp.bfloat16
MESH = pl.DeviceIdType.MESH


def nt_dot(first_op, second_op):
    return lax.dot_general(
        first_op, second_op, (((1,), (1,)), ((), ())), preferred_element_type=F32
    )


def nn_dot(first_op, second_op):
    return jnp.dot(first_op, second_op, preferred_element_type=F32)


def rounded(value):
    return value.astype(BF16).astype(F32)


def kernel(
    dims,
    state_hbm,
    cot_hbm,
    inv_hbm,
    tags_hbm,
    w_in_hbm,
    b_in_hbm,
    w_mid_hbm,
    b_mid_hbm,
    w_out_ref,
    gstate_hbm,
    gin_hbm,
    gbin_hbm,
    gmid_hbm,
    gbmid_hbm,
    gout_hbm,
    gstate_ref,
    gin_ref,
    gbin_ref,
    gbmid_ref,
    gout_ref,
    gathered,
    gathered_ext,
    state_ref,
    cot_ref,
    inv_ref,
    tags_ref,
    w_in_ref,
    b_in_ref,
    w_mid_ref,
    b_mid_ref,
    state_rows,
    grad_rows,
    adj_rows,
    back_rows,
    low_x,
    up_x,
    low_z,
    up_z,
    x_send,
    x_halo,
    z_send,
    z_halo,
    w_first,
    w_back,
    w_mid_t,
    w_mid_half,
    w_out_half,
    bias_mid,
    joint_even,
    joint_odd,
    slope_even,
    slope_odd,
    delta_even,
    delta_odd,
    totals,
    totals_in,
    totals_out,
    norm_mine,
    norm_all,
    core_send,
    core_recv,
    plane_send,
    plane_all,
    line_send,
    line_all,
    ext_core_send,
    ext_core_recv,
    ext_plane_send,
    ext_plane_all,
    ext_line_send,
    ext_line_all,
    load_sems,
    store_sems,
    norm_sems,
    halo_send_sems,
    halo_recv_sems,
    core_sems,
    plane_send_sems,
    plane_recv_sems,
    line_send_sems,
    line_recv_sems,
    ext_core_sems,
    ext_plane_send_sems,
    ext_plane_recv_sems,
    ext_line_send_sems,
    ext_line_recv_sems,
    spread_send_sems,
    spread_recv_sems,
    pair_send_sems,
    pair_recv_sems,
):
    gx, gz = dims
    channels, x_elems, z_elems, line = state_ref.shape
    hidden = w_mid_ref.shape[0]
    columns = x_elems * z_elems
    count = gx * gz
    half = hidden // 2
    n_plane, n_line = gx * 2, gz // 4
    part = hidden // n_plane
    nodes = inv_ref.shape[0]
    pieces = 4
    piece = nodes // pieces
    my_x, my_z = lax.axis_index("gx"), lax.axis_index("gz")
    me = my_x * gz + my_z
    core, side, level = my_z % 2, (my_z // 2) % 2, my_z // 4
    my_plane = my_x * 2 + side
    other_core = (my_x, my_z + 1 - 2 * core)

    loads = [
        pltpu.make_async_copy(src, dst, load_sems.at[spot])
        for spot, (src, dst) in enumerate(
            (
                (state_hbm, state_ref),
                (cot_hbm, cot_ref),
                (w_in_hbm, w_in_ref),
                (b_in_hbm, b_in_ref),
                (w_mid_hbm, w_mid_ref),
                (b_mid_hbm, b_mid_ref),
                (tags_hbm, tags_ref),
            )
        )
    ]
    inv_loads = [
        pltpu.make_async_copy(
            inv_hbm.at[pl.ds(p * piece, piece)],
            inv_ref.at[pl.ds(p * piece, piece)],
            load_sems.at[len(loads) + p],
        )
        for p in range(pieces)
    ]
    for load in loads[:2] + inv_loads + loads[2:]:
        load.start()

    barrier = pltpu.get_barrier_semaphore()

    def greet(step, carry):
        to = lax.rem(me + step, count)
        pl.semaphore_signal(
            barrier, inc=1, device_id=(to // gz, lax.rem(to, gz)), device_id_type=MESH
        )
        return carry

    lax.fori_loop(1, count, greet, 0)

    loads[0].wait()
    squares = state_ref[...] * state_ref[...]
    squares = jnp.sum(jnp.sum(squares, axis=0), axis=0)
    folded = squares[:, :128]
    for start in range(128, line, 128):
        folded = folded + squares[:, start : start + 128]
    norm_mine[...] = jnp.sum(folded, axis=0, keepdims=True)

    pl.semaphore_wait(barrier, count - 1)

    def send_norm(step, carry):
        to = lax.rem(me + step, count)
        pltpu.make_async_remote_copy(
            src_ref=norm_mine,
            dst_ref=norm_all.at[step - 1],
            send_sem=norm_sems.at[0],
            recv_sem=norm_sems.at[1],
            device_id=(to // gz, lax.rem(to, gz)),
            device_id_type=MESH,
        ).start()
        return carry

    lax.fori_loop(1, count, send_norm, 0)

    loads[1].wait()
    for c in range(channels):
        for i in range(x_elems):
            low_x[c, i * z_elems : (i + 1) * z_elems, :] = cot_ref[c, i]
    lane = lax.broadcasted_iota(jnp.int32, (columns, 128), 1)
    first_lane = lane & 64
    blocks = line // 128

    def adjoint_step(n, sums):
        spot = first_lane + n
        rows = jnp.concatenate([inv_ref[n, i] for i in range(x_elems)], axis=0)
        out = []
        for c in range(channels):
            for t in range(blocks):
                tile = low_x[c, :, t * 128 : (t + 1) * 128]
                spread = jnp.take_along_axis(tile, spot, axis=1)
                out.append(
                    sums[c * blocks + t] + rows[:, t * 128 : (t + 1) * 128] * spread
                )
        return tuple(out)

    sums = (jnp.zeros((columns, 128), F32),) * (channels * blocks)
    for p in range(pieces):
        inv_loads[p].wait()
        sums = lax.fori_loop(p * piece, (p + 1) * piece, adjoint_step, sums, unroll=4)
    for c in range(channels):
        for t in range(blocks):
            adj_rows[c, :, t * 128 : (t + 1) * 128] = sums[c * blocks + t]

    for c in range(channels):
        x_send[0, c] = adj_rows[c, 0:z_elems, :]
        x_send[1, c] = adj_rows[c, columns - z_elems : columns, :]
        for i in range(x_elems):
            z_send[0, c * x_elems + i] = adj_rows[c, i * z_elems : i * z_elems + 1, :]
            z_send[1, c * x_elems + i] = adj_rows[
                c, (i + 1) * z_elems - 1 : (i + 1) * z_elems, :
            ]
    halo_copies = []
    for spot, (src, dst, to) in enumerate(
        (
            (x_send.at[0], x_halo.at[1], (lax.rem(my_x + gx - 1, gx), my_z)),
            (x_send.at[1], x_halo.at[0], (lax.rem(my_x + 1, gx), my_z)),
            (z_send.at[0], z_halo.at[1], (my_x, lax.rem(my_z + gz - 1, gz))),
            (z_send.at[1], z_halo.at[0], (my_x, lax.rem(my_z + 1, gz))),
        )
    ):
        copy = pltpu.make_async_remote_copy(
            src_ref=src,
            dst_ref=dst,
            send_sem=halo_send_sems.at[spot],
            recv_sem=halo_recv_sems.at[spot],
            device_id=to,
            device_id_type=MESH,
        )
        copy.start()
        halo_copies.append(copy)

    for load in loads[2:]:
        load.wait()
    for i in range(x_elems):
        for k in range(z_elems):
            row = i * z_elems + k
            state_rows[row] = jnp.ones((8, line), F32)
            grad_rows[row] = jnp.zeros((16, line), F32)
            for c in range(channels):
                state_rows[row, c : c + 1, :] = state_ref[c, i, k : k + 1, :]
                grad_rows[row, c : c + 1, :] = DT_STEP * adj_rows[c, row : row + 1, :]
    w_in = w_in_ref[...]
    w_high = rounded(w_in)
    w_low = rounded(w_in - w_high)
    b_in = b_in_ref[...]
    b_high = rounded(b_in)
    b_next = rounded(b_in - b_high)
    b_last = rounded(b_in - b_high - b_next)
    joint_rows = jnp.concatenate(
        [w_high, b_high, b_next, b_last, w_high, jnp.zeros((8 - channels, hidden), F32)]
        + [w_low, jnp.zeros((16 - channels, hidden), F32)],
        axis=0,
    )
    w_first[...] = (0.5 * joint_rows).T.astype(BF16)
    w_back[...] = joint_rows[8:24].astype(BF16)
    w_mid = 0.5 * w_mid_ref[...].astype(F32)
    w_mid_half[...] = w_mid.astype(BF16)
    w_mid_t[...] = w_mid.T.astype(BF16)
    w_out_half[...] = jnp.concatenate(
        [0.5 * w_out_ref[...].astype(F32), jnp.zeros((16 - channels, hidden), F32)], axis=0
    ).T.astype(BF16)
    bias = jnp.broadcast_to(0.5 * b_mid_ref[...], (128, hidden)).T
    bias_mid[...] = bias
    totals[...] = jnp.zeros_like(totals)
    totals_in[...] = jnp.zeros_like(totals_in)
    totals_out[...] = jnp.zeros_like(totals_out)

    whole = norm_all.at[pl.ds(0, count - 1)]
    pltpu.make_async_copy(whole, whole, norm_sems.at[0]).wait()
    pltpu.make_async_copy(whole, whole, norm_sems.at[1]).wait()
    sum_squares = norm_mine[...] + jnp.sum(norm_all[0 : count - 1], axis=0)
    sum_squares = jnp.sum(sum_squares, axis=1, keepdims=True)
    entry_count = channels * columns * line * count
    inv_norm = lax.rsqrt(sum_squares / entry_count + EPS)
    row_index = lax.broadcasted_iota(jnp.int32, (8, line), 0)
    scale = jnp.where(row_index < channels, jnp.broadcast_to(inv_norm, (8, line)), 1.0)

    joints = (joint_even, joint_odd)
    slopes = (slope_even, slope_odd)
    deltas = (delta_even, delta_odd)

    def first_layer(row, turn, slot):
        scaled = state_rows[row] * scale
        high = rounded(scaled)
        low = scaled - high
        inputs = jnp.concatenate([high, low, high, jnp.zeros_like(high)], axis=0).astype(BF16)
        joints[slot][turn, hidden:, :] = inputs
        pre = nn_dot(w_first[...], inputs)
        bend = jnp.tanh(pre)
        gate = 1.0 + bend
        act = pre * gate
        slopes[slot][turn] = gate + act * (1.0 - bend)
        hidden_one = act.astype(BF16)
        joints[slot][turn, :hidden, :] = hidden_one
        return hidden_one

    def second_layer(row, hidden_one):
        pre = nn_dot(w_mid_t[...], hidden_one)
        pre = pre + jnp.concatenate([bias_mid[...]] * (line // 128), axis=1)
        bend = jnp.tanh(pre)
        gate = 1.0 + bend
        act = pre * gate
        slope_two = gate + act * (1.0 - bend)
        return act.astype(BF16), slope_two

    def last_layer(row, turn, slot, hidden_two, slope_two):
        out_grad = grad_rows[row].astype(BF16)
        back_two = nn_dot(w_out_half[...], out_grad)
        delta_two = (back_two * slope_two).astype(BF16)
        deltas[slot][turn] = delta_two
        return nt_dot(out_grad, hidden_two), nt_dot(joints[slot][turn], delta_two)

    def forward(turn, carry):
        ones = [first_layer(2 * turn + slot, turn, slot) for slot in range(2)]
        twos = [second_layer(2 * turn + slot, ones[slot]) for slot in range(2)]
        sums = [last_layer(2 * turn + slot, turn, slot, *twos[slot]) for slot in range(2)]
        totals_out[...] += sums[0][0] + sums[1][0]
        totals[...] += sums[0][1] + sums[1][1]
        return carry

    turns = columns // 2
    lax.fori_loop(0, turns, forward, 0)

    def backward(turn, carry):
        sums = []
        for slot in range(2):
            delta_one = nn_dot(w_mid_half[...], deltas[slot][turn]) * slopes[slot][turn]
            delta_one = delta_one.astype(BF16)
            sums.append(nt_dot(joints[slot][turn, hidden:, :], delta_one))
            back = nn_dot(w_back[...], delta_one)
            back = back[:8] + back[8:]
            for c in range(channels):
                back_rows[c, pl.ds(2 * turn + slot, 1), :] = back[c : c + 1, :]
        totals_in[...] += sums[0] + sums[1]
        return carry

    def plane_peer(d):
        to = lax.rem(my_plane + d, n_plane)
        return to, (to // 2, level * 4 + lax.rem(to, 2) * 2 + core)

    def line_peer(d):
        return (my_x, lax.rem(level + d, n_line) * 4 + side * 2 + core)

    def remote(src, dst, send_sem, recv_sem, to):
        copy = pltpu.make_async_remote_copy(
            src_ref=src,
            dst_ref=dst,
            send_sem=send_sem,
            recv_sem=recv_sem,
            device_id=to,
            device_id_type=MESH,
        )
        copy.start()
        return copy

    def ordered_sum(ref, size):
        return sum((ref[q] for q in range(1, size)), ref[0])

    for h in range(2):
        core_send[h] = totals[0:hidden, h * half : (h + 1) * half]
    core_copy = remote(
        core_send.at[1 - core], core_recv, core_sems.at[0], core_sems.at[1], other_core
    )
    lax.fori_loop(0, turns // 2, backward, 0)

    core_copy.wait()
    for q in range(n_plane):
        rows = slice(q * part, (q + 1) * part)
        plane_send[q] = core_send[core, rows, :] + core_recv[rows, :]
    plane_copies = []
    for d in range(1, n_plane):
        to, device = plane_peer(d)
        plane_copies.append(
            remote(
                plane_send.at[to],
                plane_all.at[my_plane],
                plane_send_sems.at[d],
                plane_recv_sems.at[d],
                device,
            )
        )
    plane_all[my_plane] = plane_send[my_plane]
    lax.fori_loop(turns // 2, turns, backward, 0)

    top = lax.broadcasted_iota(jnp.int32, (8, hidden), 0)
    mixed = jnp.where(
        top == channels + 1, totals[hidden : hidden + 8], totals_in[0:8] + totals_in[8:16]
    )
    for h in range(2):
        lanes = slice(h * half, (h + 1) * half)
        ext_core_send[h, 0:8, :] = mixed[:, lanes]
        ext_core_send[h, 8:16, :] = totals_out[0:8, lanes]
    ext_core_copy = remote(
        ext_core_send.at[1 - core],
        ext_core_recv,
        ext_core_sems.at[0],
        ext_core_sems.at[1],
        other_core,
    )

    for copy in plane_copies:
        copy.wait()
    line_send[...] = ordered_sum(plane_all, n_plane)
    line_copies = [
        remote(
            line_send,
            line_all.at[level],
            line_send_sems.at[d],
            line_recv_sems.at[d],
            line_peer(d),
        )
        for d in range(1, n_line)
    ]
    line_all[level] = line_send[...]

    ext_core_copy.wait()
    ext_plane_send[...] = ext_core_send[core] + ext_core_recv[...]
    ext_plane_copies = [
        remote(
            ext_plane_send,
            ext_plane_all.at[my_plane],
            ext_plane_send_sems.at[d],
            ext_plane_recv_sems.at[d],
            plane_peer(d)[1],
        )
        for d in range(1, n_plane)
    ]
    ext_plane_all[my_plane] = ext_plane_send[...]

    for copy in halo_copies:
        copy.wait()
    for c in range(channels):
        low_x[c, 0:z_elems, :] = x_halo[0, c]
        up_x[c, columns - z_elems : columns, :] = x_halo[1, c]
        if x_elems > 1:
            low_x[c, z_elems:columns, :] = adj_rows[c, 0 : columns - z_elems, :]
            up_x[c, 0 : columns - z_elems, :] = adj_rows[c, z_elems:columns, :]
        for i in range(x_elems):
            first, last = i * z_elems, (i + 1) * z_elems
            low_z[c, first : first + 1, :] = z_halo[0, c * x_elems + i]
            up_z[c, last - 1 : last, :] = z_halo[1, c * x_elems + i]
            if z_elems > 1:
                low_z[c, first + 1 : last, :] = adj_rows[c, first : last - 1, :]
                up_z[c, first : last - 1, :] = adj_rows[c, first + 1 : last, :]
    lane = lax.broadcasted_iota(jnp.int32, (columns, line), 1)
    row = lax.broadcasted_iota(jnp.int32, (columns, line), 0)
    spot_a, spot_b, spot_c, spot_j = (lane >> 4) & 3, (lane >> 2) & 3, lane & 3, lane >> 6
    bottom = jnp.zeros((columns, line), F32)
    ceiling = jnp.zeros((columns, line), F32)
    for i in range(x_elems):
        for k in range(z_elems):
            here = row == i * z_elems + k
            bottom = jnp.where(here, -2.0 * tags_ref[0, i, k].astype(F32), bottom)
            ceiling = jnp.where(here, -2.0 * tags_ref[1, i, k].astype(F32), ceiling)
    for c in range(channels):
        own = adj_rows[c]
        low_y = jnp.where(spot_j == 0, bottom * own, pltpu.roll(own, 52, 1) - own)
        up_y = jnp.where(
            spot_j == line // 64 - 1, ceiling * own, pltpu.roll(own, line - 52, 1) - own
        )
        jump = (
            jnp.where(spot_a == 0, pltpu.roll(low_x[c], line - 48, 1) - own, 0.0)
            + jnp.where(spot_a == 3, pltpu.roll(up_x[c], 48, 1) - own, 0.0)
            + jnp.where(spot_b == 0, low_y, 0.0)
            + jnp.where(spot_b == 3, up_y, 0.0)
            + jnp.where(spot_c == 0, pltpu.roll(low_z[c], line - 3, 1) - own, 0.0)
            + jnp.where(spot_c == 3, pltpu.roll(up_z[c], 3, 1) - own, 0.0)
        )
        back_rows[c] = own + 0.5 * KAPPA * jump + inv_norm * back_rows[c]
        for i in range(x_elems):
            gstate_ref[c, i] = back_rows[c, i * z_elems : (i + 1) * z_elems, :]
    stores = []

    def store(src, dst):
        copy = pltpu.make_async_copy(src, dst, store_sems.at[len(stores)])
        copy.start()
        stores.append(copy)

    def store_part(h, q):
        dst = gmid_hbm.at[
            pl.ds(pl.multiple_of(q * part, part), part),
            pl.ds(pl.multiple_of(h * half, half), half),
        ]
        store(gathered.at[h, q], dst)

    store(gstate_ref, gstate_hbm)

    for copy in ext_plane_copies:
        copy.wait()
    ext_line_send[...] = ordered_sum(ext_plane_all, n_plane)
    ext_line_copies = [
        remote(
            ext_line_send,
            ext_line_all.at[level],
            ext_line_send_sems.at[d],
            ext_line_recv_sems.at[d],
            line_peer(d),
        )
        for d in range(1, n_line)
    ]
    ext_line_all[level] = ext_line_send[...]

    def to_pair(slot, d):
        return remote(
            gathered.at[core, slot],
            gathered.at[core, slot],
            pair_send_sems.at[d],
            pair_recv_sems.at[d],
            other_core,
        )

    factor = 4.0 / math.sqrt(entry_count // channels)
    for copy in line_copies:
        copy.wait()
    gathered[core, my_plane] = factor * ordered_sum(line_all, n_line)
    spread_copies = [
        remote(
            gathered.at[core, my_plane],
            gathered.at[core, my_plane],
            spread_send_sems.at[d],
            spread_recv_sems.at[d],
            plane_peer(d)[1],
        )
        for d in range(1, n_plane)
    ]
    pair_copies = [to_pair(my_plane, 0)]
    store_part(core, my_plane)
    for copy in ext_line_copies:
        copy.wait()
    gathered_ext[core] = factor * ordered_sum(ext_line_all, n_line)
    ext_pair_copy = remote(
        gathered_ext.at[core],
        gathered_ext.at[core],
        pair_send_sems.at[n_plane],
        pair_recv_sems.at[n_plane],
        other_core,
    )
    for d in range(1, n_plane):
        spread_copies[d - 1].wait_recv()
        slot = lax.rem(my_plane + n_plane - d, n_plane)
        pair_copies.append(to_pair(slot, d))
        store_part(core, slot)
    ext_pair_copy.wait()
    for h in range(2):
        lanes = slice(h * half, (h + 1) * half)
        gin_ref[:, lanes] = gathered_ext[h, 0:channels]
        gbin_ref[:, lanes] = gathered_ext[h, channels : channels + 1]
        gbmid_ref[:, lanes] = gathered_ext[h, channels + 1 : channels + 2]
        gout_ref[:, lanes] = gathered_ext[h, 8 : 8 + channels]
    store(gin_ref, gin_hbm)
    store(gbin_ref, gbin_hbm)
    store(gbmid_ref, gbmid_hbm)
    store(gout_ref, gout_hbm)
    for d in range(n_plane):
        pair_copies[d].wait()
        store_part(1 - core, lax.rem(my_plane + n_plane - d, n_plane))
    for copy in spread_copies:
        copy.wait_send()
    for copy in stores:
        copy.wait()


def writer(*refs):
    half = len(refs) // 2
    copies = [
        pltpu.make_async_copy(src, dst, refs[-1].at[spot])
        for spot, (src, dst) in enumerate(zip(refs[:half], refs[half:-1]))
    ]
    for copy in copies:
        copy.start()
    for copy in copies:
        copy.wait()


def per_device(dims, state, cotangent, local_inverse, wall_tags, w_in, b_in, w_mid, b_mid, w_out):
    gx, gz = dims
    channels, x_elems, z_elems, line = state.shape
    hidden = w_mid.shape[0]
    columns = x_elems * z_elems
    n_plane, n_line = gx * 2, gz // 4
    part = hidden // n_plane
    half = hidden // 2
    turns = columns // 2
    vmem = pl.BlockSpec(memory_space=pltpu.VMEM)
    hbm = pl.BlockSpec(memory_space=pltpu.HBM)
    rows = pltpu.VMEM((channels, columns, line), F32)
    dma = pltpu.SemaphoreType.DMA

    def same(array):
        return pltpu.VMEM(array.shape, array.dtype)

    b_in, b_mid = b_in.reshape(1, hidden), b_mid.reshape(1, hidden)
    out_shape = (
        jax.ShapeDtypeStruct(state.shape, F32),
        jax.ShapeDtypeStruct((channels, hidden), F32),
        jax.ShapeDtypeStruct((1, hidden), F32),
        jax.ShapeDtypeStruct((hidden, hidden), F32),
        jax.ShapeDtypeStruct((1, hidden), F32),
        jax.ShapeDtypeStruct((channels, hidden), F32),
    )
    out = pl.pallas_call(
        functools.partial(kernel, dims),
        out_shape=out_shape,
        in_specs=[hbm] * 8 + [vmem],
        out_specs=(hbm,) * 6,
        scratch_shapes=[
            same(state),
            pltpu.VMEM((channels, hidden), F32),
            pltpu.VMEM((1, hidden), F32),
            pltpu.VMEM((1, hidden), F32),
            pltpu.VMEM((channels, hidden), F32),
            pltpu.VMEM((2, n_plane, part, half), F32),
            pltpu.VMEM((2, 16, half), F32),
            same(state),
            same(cotangent),
            same(local_inverse),
            pltpu.SMEM(wall_tags.shape, jnp.int32),
            same(w_in),
            same(b_in),
            same(w_mid),
            same(b_mid),
            pltpu.VMEM((columns, 8, line), F32),
            pltpu.VMEM((columns, 16, line), F32),
            rows,
            rows,
            rows,
            rows,
            rows,
            rows,
            pltpu.VMEM((2, channels, z_elems, line), F32),
            pltpu.VMEM((2, channels, z_elems, line), F32),
            pltpu.VMEM((2, channels * x_elems, 1, line), F32),
            pltpu.VMEM((2, channels * x_elems, 1, line), F32),
            pltpu.VMEM((hidden, 32), BF16),
            pltpu.VMEM((16, hidden), BF16),
            pltpu.VMEM((hidden, hidden), BF16),
            pltpu.VMEM((hidden, hidden), BF16),
            pltpu.VMEM((hidden, 16), BF16),
            pltpu.VMEM((hidden, 128), F32),
            pltpu.VMEM((turns, hidden + 32, line), BF16),
            pltpu.VMEM((turns, hidden + 32, line), BF16),
            pltpu.VMEM((turns, hidden, line), F32),
            pltpu.VMEM((turns, hidden, line), F32),
            pltpu.VMEM((turns, hidden, line), BF16),
            pltpu.VMEM((turns, hidden, line), BF16),
            pltpu.VMEM((hidden + 32, hidden), F32),
            pltpu.VMEM((32, hidden), F32),
            pltpu.VMEM((16, hidden), F32),
            pltpu.VMEM((1, 128), F32),
            pltpu.VMEM((gx * gz, 1, 128), F32),
            pltpu.VMEM((2, hidden, half), F32),
            pltpu.VMEM((hidden, half), F32),
            pltpu.VMEM((n_plane, part, half), F32),
            pltpu.VMEM((n_plane, part, half), F32),
            pltpu.VMEM((part, half), F32),
            pltpu.VMEM((n_line, part, half), F32),
            pltpu.VMEM((2, 16, half), F32),
            pltpu.VMEM((16, half), F32),
            pltpu.VMEM((16, half), F32),
            pltpu.VMEM((n_plane, 16, half), F32),
            pltpu.VMEM((16, half), F32),
            pltpu.VMEM((n_line, 16, half), F32),
            dma((11,)),
            dma((2 * n_plane + 5,)),
            dma((2,)),
            dma((4,)),
            dma((4,)),
            dma((2,)),
            dma((n_plane,)),
            dma((n_plane,)),
            dma((n_line,)),
            dma((n_line,)),
            dma((2,)),
            dma((n_plane,)),
            dma((n_plane,)),
            dma((n_line,)),
            dma((n_line,)),
            dma((n_plane,)),
            dma((n_plane,)),
            dma((n_plane + 1,)),
            dma((n_plane + 1,)),
        ],
        compiler_params=pltpu.CompilerParams(
            collective_id=0, has_side_effects=True, vmem_limit_bytes=62 * 1024 * 1024
        ),
    )(state, cotangent, local_inverse, wall_tags, w_in, b_in, w_mid, b_mid, w_out.T)
    out = pl.pallas_call(
        writer,
        out_shape=out_shape,
        in_specs=[hbm] * 6,
        out_specs=(hbm,) * 6,
        scratch_shapes=[dma((6,))],
        compiler_params=pltpu.CompilerParams(vmem_limit_bytes=62 * 1024 * 1024),
    )(*out)
    return out[0], out[1], out[2].reshape(hidden), out[3], out[4].reshape(hidden), out[5].T


def solution(mesh):
    placed = (
        P(None, "gx", "gz", None),
        P(None, "gx", "gz", None),
        P(None, "gx", "gz", None),
        P(None, "gx", "gz"),
        P(),
        P(),
        P(),
        P(),
        P(),
    )
    return jax.shard_map(
        functools.partial(per_device, (mesh.shape["gx"], mesh.shape["gz"])),
        mesh=mesh,
        in_specs=placed,
        out_specs=(P(None, "gx", "gz", None), P(), P(), P(), P(), P()),
        check_vma=False,
    )
```

```python
import functools
import math

import jax
import jax.numpy as jnp
from jax import lax
from jax.experimental import pallas as pl
from jax.experimental.pallas import tpu as pltpu
from jax.sharding import PartitionSpec as P

KAPPA = 0.5
DT_STEP = 0.5
EPS = 1e-06
F32 = jnp.float32
BF16 = jnp.bfloat16
MESH = pl.DeviceIdType.MESH


def nt_dot(first_op, second_op):
    return lax.dot_general(
        first_op, second_op, (((1,), (1,)), ((), ())), preferred_element_type=F32
    )


def nn_dot(first_op, second_op):
    return jnp.dot(first_op, second_op, preferred_element_type=F32)


def rounded(value):
    return value.astype(BF16).astype(F32)


def kernel(
    dims,
    state_hbm,
    cot_hbm,
    inv_hbm,
    tags_hbm,
    w_in_hbm,
    b_in_hbm,
    w_mid_hbm,
    b_mid_hbm,
    w_out_ref,
    gstate_hbm,
    gin_hbm,
    gbin_hbm,
    gmid_hbm,
    gbmid_hbm,
    gout_hbm,
    gstate_ref,
    gin_ref,
    gbin_ref,
    gbmid_ref,
    gout_ref,
    gathered,
    gathered_ext,
    state_ref,
    cot_ref,
    inv_ref,
    tags_ref,
    w_in_ref,
    b_in_ref,
    w_mid_ref,
    b_mid_ref,
    state_rows,
    grad_rows,
    adj_rows,
    back_rows,
    low_x,
    up_x,
    low_z,
    up_z,
    x_send,
    x_halo,
    z_send,
    z_halo,
    w_first,
    w_back,
    w_mid_t,
    w_mid_half,
    w_out_half,
    bias_mid,
    joints,
    slopes,
    deltas,
    totals,
    totals_in,
    totals_out,
    norm_mine,
    norm_all,
    core_send,
    core_recv,
    plane_send,
    plane_all,
    line_send,
    line_all,
    ext_core_send,
    ext_core_recv,
    ext_plane_send,
    ext_plane_all,
    ext_line_send,
    ext_line_all,
    load_sems,
    store_sems,
    norm_sems,
    halo_send_sems,
    halo_recv_sems,
    core_sems,
    plane_send_sems,
    plane_recv_sems,
    line_send_sems,
    line_recv_sems,
    ext_core_sems,
    ext_plane_send_sems,
    ext_plane_recv_sems,
    ext_line_send_sems,
    ext_line_recv_sems,
    spread_send_sems,
    spread_recv_sems,
    pair_send_sems,
    pair_recv_sems,
):
    gx, gz = dims
    channels, x_elems, z_elems, line = state_ref.shape
    hidden = w_mid_ref.shape[0]
    columns = x_elems * z_elems
    count = gx * gz
    half = hidden // 2
    n_plane, n_line = gx * 2, gz // 4
    part = hidden // n_plane
    nodes = inv_ref.shape[0]
    pieces = 4
    piece = nodes // pieces
    my_x, my_z = lax.axis_index("gx"), lax.axis_index("gz")
    me = my_x * gz + my_z
    core, side, level = my_z % 2, (my_z // 2) % 2, my_z // 4
    my_plane = my_x * 2 + side
    other_core = (my_x, my_z + 1 - 2 * core)

    loads = [
        pltpu.make_async_copy(src, dst, load_sems.at[spot])
        for spot, (src, dst) in enumerate(
            (
                (state_hbm, state_ref),
                (cot_hbm, cot_ref),
                (w_in_hbm, w_in_ref),
                (b_in_hbm, b_in_ref),
                (w_mid_hbm, w_mid_ref),
                (b_mid_hbm, b_mid_ref),
                (tags_hbm, tags_ref),
            )
        )
    ]
    inv_loads = [
        pltpu.make_async_copy(
            inv_hbm.at[pl.ds(p * piece, piece)],
            inv_ref.at[pl.ds(p * piece, piece)],
            load_sems.at[len(loads) + p],
        )
        for p in range(pieces)
    ]
    for load in loads[2:] + loads[:2] + inv_loads:
        load.start()

    barrier = pltpu.get_barrier_semaphore()

    def greet(step, carry):
        to = lax.rem(me + step, count)
        pl.semaphore_signal(
            barrier, inc=1, device_id=(to // gz, lax.rem(to, gz)), device_id_type=MESH
        )
        return carry

    lax.fori_loop(1, count, greet, 0)

    for load in loads[2:]:
        load.wait()
    w_in = w_in_ref[...]
    w_high = rounded(w_in)
    w_low = rounded(w_in - w_high)
    b_in = b_in_ref[...]
    b_high = rounded(b_in)
    b_next = rounded(b_in - b_high)
    b_last = rounded(b_in - b_high - b_next)
    joint_rows = jnp.concatenate(
        [w_high, b_high, b_next, b_last, w_high, jnp.zeros((8 - channels, hidden), F32)]
        + [w_low, jnp.zeros((16 - channels, hidden), F32)],
        axis=0,
    )
    w_first[...] = (0.5 * joint_rows).T.astype(BF16)
    w_back[...] = joint_rows[8:24].astype(BF16)
    w_mid = 0.5 * w_mid_ref[...].astype(F32)
    w_mid_half[...] = w_mid.astype(BF16)
    w_mid_t[...] = w_mid.T.astype(BF16)
    w_out_half[...] = jnp.concatenate(
        [0.5 * w_out_ref[...].astype(F32), jnp.zeros((16 - channels, hidden), F32)], axis=0
    ).T.astype(BF16)
    bias = jnp.broadcast_to(0.5 * b_mid_ref[...], (128, hidden)).T
    bias_mid[...] = bias
    totals[...] = jnp.zeros_like(totals)
    totals_in[...] = jnp.zeros_like(totals_in)
    totals_out[...] = jnp.zeros_like(totals_out)

    loads[0].wait()
    squares = state_ref[...] * state_ref[...]
    squares = jnp.sum(jnp.sum(squares, axis=0), axis=0)
    folded = squares[:, :128]
    for start in range(128, line, 128):
        folded = folded + squares[:, start : start + 128]
    norm_mine[...] = jnp.sum(folded, axis=0, keepdims=True)

    pl.semaphore_wait(barrier, count - 1)

    def send_norm(step, carry):
        to = lax.rem(me + step, count)
        pltpu.make_async_remote_copy(
            src_ref=norm_mine,
            dst_ref=norm_all.at[step - 1],
            send_sem=norm_sems.at[0],
            recv_sem=norm_sems.at[1],
            device_id=(to // gz, lax.rem(to, gz)),
            device_id_type=MESH,
        ).start()
        return carry

    lax.fori_loop(1, count, send_norm, 0)

    loads[1].wait()
    for c in range(channels):
        for i in range(x_elems):
            low_x[c, i * z_elems : (i + 1) * z_elems, :] = cot_ref[c, i]
    lane = lax.broadcasted_iota(jnp.int32, (columns, 128), 1)
    first_lane = lane & 64
    blocks = line // 128

    def adjoint_step(n, sums):
        spot = first_lane + n
        rows = jnp.concatenate([inv_ref[n, i] for i in range(x_elems)], axis=0)
        out = []
        for c in range(channels):
            for t in range(blocks):
                tile = low_x[c, :, t * 128 : (t + 1) * 128]
                spread = jnp.take_along_axis(tile, spot, axis=1)
                out.append(
                    sums[c * blocks + t] + rows[:, t * 128 : (t + 1) * 128] * spread
                )
        return tuple(out)

    sums = (jnp.zeros((columns, 128), F32),) * (channels * blocks)
    for p in range(pieces):
        inv_loads[p].wait()
        sums = lax.fori_loop(p * piece, (p + 1) * piece, adjoint_step, sums, unroll=piece)
    for c in range(channels):
        for t in range(blocks):
            adj_rows[c, :, t * 128 : (t + 1) * 128] = sums[c * blocks + t]

    for c in range(channels):
        x_send[0, c] = adj_rows[c, 0:z_elems, :]
        x_send[1, c] = adj_rows[c, columns - z_elems : columns, :]
        for i in range(x_elems):
            z_send[0, c * x_elems + i] = adj_rows[c, i * z_elems : i * z_elems + 1, :]
            z_send[1, c * x_elems + i] = adj_rows[
                c, (i + 1) * z_elems - 1 : (i + 1) * z_elems, :
            ]
    halo_copies = []
    for spot, (src, dst, to) in enumerate(
        (
            (x_send.at[0], x_halo.at[1], (lax.rem(my_x + gx - 1, gx), my_z)),
            (x_send.at[1], x_halo.at[0], (lax.rem(my_x + 1, gx), my_z)),
            (z_send.at[0], z_halo.at[1], (my_x, lax.rem(my_z + gz - 1, gz))),
            (z_send.at[1], z_halo.at[0], (my_x, lax.rem(my_z + 1, gz))),
        )
    ):
        copy = pltpu.make_async_remote_copy(
            src_ref=src,
            dst_ref=dst,
            send_sem=halo_send_sems.at[spot],
            recv_sem=halo_recv_sems.at[spot],
            device_id=to,
            device_id_type=MESH,
        )
        copy.start()
        halo_copies.append(copy)

    for i in range(x_elems):
        for k in range(z_elems):
            row = i * z_elems + k
            state_rows[row] = jnp.ones((8, line), F32)
            grad_rows[row] = jnp.zeros((16, line), F32)
            for c in range(channels):
                state_rows[row, c : c + 1, :] = state_ref[c, i, k : k + 1, :]
                grad_rows[row, c : c + 1, :] = DT_STEP * adj_rows[c, row : row + 1, :]
    whole = norm_all.at[pl.ds(0, count - 1)]
    pltpu.make_async_copy(whole, whole, norm_sems.at[0]).wait()
    pltpu.make_async_copy(whole, whole, norm_sems.at[1]).wait()
    sum_squares = norm_mine[...] + jnp.sum(norm_all[0 : count - 1], axis=0)
    sum_squares = jnp.sum(sum_squares, axis=1, keepdims=True)
    entry_count = channels * columns * line * count
    inv_norm = lax.rsqrt(sum_squares / entry_count + EPS)
    row_index = lax.broadcasted_iota(jnp.int32, (8, line), 0)
    scale = jnp.where(row_index < channels, jnp.broadcast_to(inv_norm, (8, line)), 1.0)

    def first_layer(row):
        scaled = state_rows[row] * scale
        high = rounded(scaled)
        low = scaled - high
        inputs = jnp.concatenate([high, low, high, jnp.zeros_like(high)], axis=0).astype(BF16)
        joints[row, hidden:, :] = inputs
        pre = nn_dot(w_first[...], inputs)
        bend = jnp.tanh(pre)
        gate = 1.0 + bend
        act = pre * gate
        slopes[row] = gate + act * (1.0 - bend)
        joints[row, :hidden, :] = act.astype(BF16)

    def second_layer(row):
        pre = nn_dot(w_mid_t[...], joints[row, :hidden, :])
        pre = pre + jnp.concatenate([bias_mid[...]] * (line // 128), axis=1)
        bend = jnp.tanh(pre)
        gate = 1.0 + bend
        act = pre * gate
        slope_two = gate + act * (1.0 - bend)
        out_grad = grad_rows[row].astype(BF16)
        totals_out[...] += nt_dot(out_grad, act.astype(BF16))
        back_two = nn_dot(w_out_half[...], out_grad)
        deltas[row] = (back_two * slope_two).astype(BF16)

    def last_layer(row):
        totals[...] += nt_dot(joints[row], deltas[row])

    for step in range(columns + 2):
        if step < columns:
            first_layer(step)
        if 1 <= step <= columns:
            second_layer(step - 1)
        if step >= 2:
            last_layer(step - 2)

    def backward(row):
        delta_one = nn_dot(w_mid_half[...], deltas[row]) * slopes[row]
        delta_one = delta_one.astype(BF16)
        totals_in[...] += nt_dot(joints[row, hidden:, :], delta_one)
        back = nn_dot(w_back[...], delta_one)
        back = back[:8] + back[8:]
        for c in range(channels):
            back_rows[c, row : row + 1, :] = back[c : c + 1, :]

    def plane_peer(d):
        to = lax.rem(my_plane + d, n_plane)
        return to, (to // 2, level * 4 + lax.rem(to, 2) * 2 + core)

    def line_peer(d):
        return (my_x, lax.rem(level + d, n_line) * 4 + side * 2 + core)

    def remote(src, dst, send_sem, recv_sem, to):
        copy = pltpu.make_async_remote_copy(
            src_ref=src,
            dst_ref=dst,
            send_sem=send_sem,
            recv_sem=recv_sem,
            device_id=to,
            device_id_type=MESH,
        )
        copy.start()
        return copy

    def ordered_sum(ref, size):
        return sum((ref[q] for q in range(1, size)), ref[0])

    for h in range(2):
        core_send[h] = totals[0:hidden, h * half : (h + 1) * half]
    core_copy = remote(
        core_send.at[1 - core], core_recv, core_sems.at[0], core_sems.at[1], other_core
    )
    for row in range(columns // 2):
        backward(row)

    core_copy.wait()
    for q in range(n_plane):
        rows = slice(q * part, (q + 1) * part)
        plane_send[q] = core_send[core, rows, :] + core_recv[rows, :]
    plane_copies = []
    for d in range(1, n_plane):
        to, device = plane_peer(d)
        plane_copies.append(
            remote(
                plane_send.at[to],
                plane_all.at[my_plane],
                plane_send_sems.at[d],
                plane_recv_sems.at[d],
                device,
            )
        )
    plane_all[my_plane] = plane_send[my_plane]
    for row in range(columns // 2, columns):
        backward(row)

    top = lax.broadcasted_iota(jnp.int32, (8, hidden), 0)
    mixed = jnp.where(
        top == channels + 1, totals[hidden : hidden + 8], totals_in[0:8] + totals_in[8:16]
    )
    for h in range(2):
        lanes = slice(h * half, (h + 1) * half)
        ext_core_send[h, 0:8, :] = mixed[:, lanes]
        ext_core_send[h, 8:16, :] = totals_out[0:8, lanes]
    ext_core_copy = remote(
        ext_core_send.at[1 - core],
        ext_core_recv,
        ext_core_sems.at[0],
        ext_core_sems.at[1],
        other_core,
    )

    for copy in plane_copies:
        copy.wait()
    line_send[...] = ordered_sum(plane_all, n_plane)
    line_copies = [
        remote(
            line_send,
            line_all.at[level],
            line_send_sems.at[d],
            line_recv_sems.at[d],
            line_peer(d),
        )
        for d in range(1, n_line)
    ]
    line_all[level] = line_send[...]

    ext_core_copy.wait()
    ext_plane_send[...] = ext_core_send[core] + ext_core_recv[...]
    ext_plane_copies = [
        remote(
            ext_plane_send,
            ext_plane_all.at[my_plane],
            ext_plane_send_sems.at[d],
            ext_plane_recv_sems.at[d],
            plane_peer(d)[1],
        )
        for d in range(1, n_plane)
    ]
    ext_plane_all[my_plane] = ext_plane_send[...]

    for copy in halo_copies:
        copy.wait()
    for c in range(channels):
        low_x[c, 0:z_elems, :] = x_halo[0, c]
        up_x[c, columns - z_elems : columns, :] = x_halo[1, c]
        if x_elems > 1:
            low_x[c, z_elems:columns, :] = adj_rows[c, 0 : columns - z_elems, :]
            up_x[c, 0 : columns - z_elems, :] = adj_rows[c, z_elems:columns, :]
        for i in range(x_elems):
            first, last = i * z_elems, (i + 1) * z_elems
            low_z[c, first : first + 1, :] = z_halo[0, c * x_elems + i]
            up_z[c, last - 1 : last, :] = z_halo[1, c * x_elems + i]
            if z_elems > 1:
                low_z[c, first + 1 : last, :] = adj_rows[c, first : last - 1, :]
                up_z[c, first : last - 1, :] = adj_rows[c, first + 1 : last, :]
    lane = lax.broadcasted_iota(jnp.int32, (columns, line), 1)
    row = lax.broadcasted_iota(jnp.int32, (columns, line), 0)
    spot_a, spot_b, spot_c, spot_j = (lane >> 4) & 3, (lane >> 2) & 3, lane & 3, lane >> 6
    bottom = jnp.zeros((columns, line), F32)
    ceiling = jnp.zeros((columns, line), F32)
    for i in range(x_elems):
        for k in range(z_elems):
            here = row == i * z_elems + k
            bottom = jnp.where(here, -2.0 * tags_ref[0, i, k].astype(F32), bottom)
            ceiling = jnp.where(here, -2.0 * tags_ref[1, i, k].astype(F32), ceiling)
    for c in range(channels):
        own = adj_rows[c]
        low_y = jnp.where(spot_j == 0, bottom * own, pltpu.roll(own, 52, 1) - own)
        up_y = jnp.where(
            spot_j == line // 64 - 1, ceiling * own, pltpu.roll(own, line - 52, 1) - own
        )
        jump = (
            jnp.where(spot_a == 0, pltpu.roll(low_x[c], line - 48, 1) - own, 0.0)
            + jnp.where(spot_a == 3, pltpu.roll(up_x[c], 48, 1) - own, 0.0)
            + jnp.where(spot_b == 0, low_y, 0.0)
            + jnp.where(spot_b == 3, up_y, 0.0)
            + jnp.where(spot_c == 0, pltpu.roll(low_z[c], line - 3, 1) - own, 0.0)
            + jnp.where(spot_c == 3, pltpu.roll(up_z[c], 3, 1) - own, 0.0)
        )
        back_rows[c] = own + 0.5 * KAPPA * jump + inv_norm * back_rows[c]
        for i in range(x_elems):
            gstate_ref[c, i] = back_rows[c, i * z_elems : (i + 1) * z_elems, :]
    stores = []

    def store(src, dst):
        copy = pltpu.make_async_copy(src, dst, store_sems.at[len(stores)])
        copy.start()
        stores.append(copy)

    def store_part(h, q):
        dst = gmid_hbm.at[
            pl.ds(pl.multiple_of(q * part, part), part),
            pl.ds(pl.multiple_of(h * half, half), half),
        ]
        store(gathered.at[h, q], dst)

    store(gstate_ref, gstate_hbm)

    for copy in ext_plane_copies:
        copy.wait()
    ext_line_send[...] = ordered_sum(ext_plane_all, n_plane)
    ext_line_copies = [
        remote(
            ext_line_send,
            ext_line_all.at[level],
            ext_line_send_sems.at[d],
            ext_line_recv_sems.at[d],
            line_peer(d),
        )
        for d in range(1, n_line)
    ]
    ext_line_all[level] = ext_line_send[...]

    def to_pair(slot, d):
        return remote(
            gathered.at[core, slot],
            gathered.at[core, slot],
            pair_send_sems.at[d],
            pair_recv_sems.at[d],
            other_core,
        )

    factor = 4.0 / math.sqrt(entry_count // channels)
    for copy in line_copies:
        copy.wait()
    gathered[core, my_plane] = factor * ordered_sum(line_all, n_line)
    spread_copies = [
        remote(
            gathered.at[core, my_plane],
            gathered.at[core, my_plane],
            spread_send_sems.at[d],
            spread_recv_sems.at[d],
            plane_peer(d)[1],
        )
        for d in range(1, n_plane)
    ]
    pair_copies = [to_pair(my_plane, 0)]
    store_part(core, my_plane)
    for copy in ext_line_copies:
        copy.wait()
    gathered_ext[core] = factor * ordered_sum(ext_line_all, n_line)
    ext_pair_copy = remote(
        gathered_ext.at[core],
        gathered_ext.at[core],
        pair_send_sems.at[n_plane],
        pair_recv_sems.at[n_plane],
        other_core,
    )
    for d in range(1, n_plane):
        spread_copies[d - 1].wait_recv()
        slot = lax.rem(my_plane + n_plane - d, n_plane)
        pair_copies.append(to_pair(slot, d))
        store_part(core, slot)
    ext_pair_copy.wait()
    for h in range(2):
        lanes = slice(h * half, (h + 1) * half)
        gin_ref[:, lanes] = gathered_ext[h, 0:channels]
        gbin_ref[:, lanes] = gathered_ext[h, channels : channels + 1]
        gbmid_ref[:, lanes] = gathered_ext[h, channels + 1 : channels + 2]
        gout_ref[:, lanes] = gathered_ext[h, 8 : 8 + channels]
    store(gin_ref, gin_hbm)
    store(gbin_ref, gbin_hbm)
    store(gbmid_ref, gbmid_hbm)
    store(gout_ref, gout_hbm)
    for d in range(n_plane):
        pair_copies[d].wait()
        store_part(1 - core, lax.rem(my_plane + n_plane - d, n_plane))
    for copy in spread_copies:
        copy.wait_send()
    for copy in stores:
        copy.wait()


def writer(*refs):
    size = (len(refs) - 1) // 3
    sems = refs[-1]
    sources, results, held = refs[:size], refs[size : 2 * size], refs[2 * size : -1]
    loads = [
        pltpu.make_async_copy(sources[spot], held[spot], sems.at[spot]) for spot in range(size)
    ]
    stores = [
        pltpu.make_async_copy(held[spot], results[spot], sems.at[size + spot])
        for spot in range(size)
    ]
    for load in loads:
        load.start()
    for load, store in zip(loads, stores):
        load.wait()
        store.start()
    for store in stores:
        store.wait()


def per_device(dims, state, cotangent, local_inverse, wall_tags, w_in, b_in, w_mid, b_mid, w_out):
    gx, gz = dims
    channels, x_elems, z_elems, line = state.shape
    hidden = w_mid.shape[0]
    columns = x_elems * z_elems
    n_plane, n_line = gx * 2, gz // 4
    part = hidden // n_plane
    half = hidden // 2
    vmem = pl.BlockSpec(memory_space=pltpu.VMEM)
    hbm = pl.BlockSpec(memory_space=pltpu.HBM)
    rows = pltpu.VMEM((channels, columns, line), F32)
    dma = pltpu.SemaphoreType.DMA

    def same(array):
        return pltpu.VMEM(array.shape, array.dtype)

    b_in, b_mid = b_in.reshape(1, hidden), b_mid.reshape(1, hidden)
    out_shape = (
        jax.ShapeDtypeStruct(state.shape, F32),
        jax.ShapeDtypeStruct((channels, hidden), F32),
        jax.ShapeDtypeStruct((1, hidden), F32),
        jax.ShapeDtypeStruct((hidden, hidden), F32),
        jax.ShapeDtypeStruct((1, hidden), F32),
        jax.ShapeDtypeStruct((channels, hidden), F32),
    )
    out = pl.pallas_call(
        functools.partial(kernel, dims),
        out_shape=out_shape,
        in_specs=[hbm] * 8 + [vmem],
        out_specs=(hbm,) * 6,
        scratch_shapes=[
            same(state),
            pltpu.VMEM((channels, hidden), F32),
            pltpu.VMEM((1, hidden), F32),
            pltpu.VMEM((1, hidden), F32),
            pltpu.VMEM((channels, hidden), F32),
            pltpu.VMEM((2, n_plane, part, half), F32),
            pltpu.VMEM((2, 16, half), F32),
            same(state),
            same(cotangent),
            same(local_inverse),
            pltpu.SMEM(wall_tags.shape, jnp.int32),
            same(w_in),
            same(b_in),
            same(w_mid),
            same(b_mid),
            pltpu.VMEM((columns, 8, line), F32),
            pltpu.VMEM((columns, 16, line), F32),
            rows,
            rows,
            rows,
            rows,
            rows,
            rows,
            pltpu.VMEM((2, channels, z_elems, line), F32),
            pltpu.VMEM((2, channels, z_elems, line), F32),
            pltpu.VMEM((2, channels * x_elems, 1, line), F32),
            pltpu.VMEM((2, channels * x_elems, 1, line), F32),
            pltpu.VMEM((hidden, 32), BF16),
            pltpu.VMEM((16, hidden), BF16),
            pltpu.VMEM((hidden, hidden), BF16),
            pltpu.VMEM((hidden, hidden), BF16),
            pltpu.VMEM((hidden, 16), BF16),
            pltpu.VMEM((hidden, 128), F32),
            pltpu.VMEM((columns, hidden + 32, line), BF16),
            pltpu.VMEM((columns, hidden, line), F32),
            pltpu.VMEM((columns, hidden, line), BF16),
            pltpu.VMEM((hidden + 32, hidden), F32),
            pltpu.VMEM((32, hidden), F32),
            pltpu.VMEM((16, hidden), F32),
            pltpu.VMEM((1, 128), F32),
            pltpu.VMEM((gx * gz, 1, 128), F32),
            pltpu.VMEM((2, hidden, half), F32),
            pltpu.VMEM((hidden, half), F32),
            pltpu.VMEM((n_plane, part, half), F32),
            pltpu.VMEM((n_plane, part, half), F32),
            pltpu.VMEM((part, half), F32),
            pltpu.VMEM((n_line, part, half), F32),
            pltpu.VMEM((2, 16, half), F32),
            pltpu.VMEM((16, half), F32),
            pltpu.VMEM((16, half), F32),
            pltpu.VMEM((n_plane, 16, half), F32),
            pltpu.VMEM((16, half), F32),
            pltpu.VMEM((n_line, 16, half), F32),
            dma((11,)),
            dma((2 * n_plane + 5,)),
            dma((2,)),
            dma((4,)),
            dma((4,)),
            dma((2,)),
            dma((n_plane,)),
            dma((n_plane,)),
            dma((n_line,)),
            dma((n_line,)),
            dma((2,)),
            dma((n_plane,)),
            dma((n_plane,)),
            dma((n_line,)),
            dma((n_line,)),
            dma((n_plane,)),
            dma((n_plane,)),
            dma((n_plane + 1,)),
            dma((n_plane + 1,)),
        ],
        compiler_params=pltpu.CompilerParams(
            collective_id=0, has_side_effects=True, vmem_limit_bytes=62 * 1024 * 1024
        ),
    )(state, cotangent, local_inverse, wall_tags, w_in, b_in, w_mid, b_mid, w_out.T)
    out = pl.pallas_call(
        writer,
        out_shape=out_shape,
        in_specs=[hbm] * 6,
        out_specs=(hbm,) * 6,
        scratch_shapes=[pltpu.VMEM(o.shape, F32) for o in out_shape] + [dma((12,))],
        compiler_params=pltpu.CompilerParams(vmem_limit_bytes=62 * 1024 * 1024),
    )(*out)
    return out[0], out[1], out[2].reshape(hidden), out[3], out[4].reshape(hidden), out[5].T


def solution(mesh):
    placed = (
        P(None, "gx", "gz", None),
        P(None, "gx", "gz", None),
        P(None, "gx", "gz", None),
        P(None, "gx", "gz"),
        P(),
        P(),
        P(),
        P(),
        P(),
    )
    return jax.shard_map(
        functools.partial(per_device, (mesh.shape["gx"], mesh.shape["gz"])),
        mesh=mesh,
        in_specs=placed,
        out_specs=(P(None, "gx", "gz", None), P(), P(), P(), P(), P()),
        check_vma=False,
    )
```

```python
import functools
import math

import jax
import jax.numpy as jnp
from jax import lax
from jax.experimental import pallas as pl
from jax.experimental.pallas import tpu as pltpu
from jax.sharding import PartitionSpec as P

KAPPA = 0.5
DT_STEP = 0.5
EPS = 1e-06
F32 = jnp.float32
BF16 = jnp.bfloat16
MESH = pl.DeviceIdType.MESH


def nt_dot(first_op, second_op):
    return lax.dot_general(
        first_op, second_op, (((1,), (1,)), ((), ())), preferred_element_type=F32
    )


def nn_dot(first_op, second_op):
    return jnp.dot(first_op, second_op, preferred_element_type=F32)


def rounded(value):
    return value.astype(BF16).astype(F32)


def kernel(
    dims,
    state_hbm,
    cot_hbm,
    inv_hbm,
    tags_hbm,
    w_in_hbm,
    b_in_hbm,
    w_mid_hbm,
    b_mid_hbm,
    w_out_ref,
    gstate_hbm,
    gin_hbm,
    gbin_hbm,
    gmid_hbm,
    gbmid_hbm,
    gout_hbm,
    gstate_ref,
    gin_ref,
    gbin_ref,
    gbmid_ref,
    gout_ref,
    gathered,
    gathered_ext,
    state_ref,
    cot_ref,
    inv_ref,
    tags_ref,
    w_in_ref,
    b_in_ref,
    w_mid_ref,
    b_mid_ref,
    state_rows,
    grad_rows,
    adj_rows,
    back_rows,
    low_x,
    up_x,
    low_z,
    up_z,
    x_send,
    x_halo,
    z_send,
    z_halo,
    w_first,
    w_back,
    w_mid_t,
    w_mid_half,
    w_out_half,
    bias_mid,
    joints,
    bends,
    hiddens,
    deltas,
    totals,
    totals_in,
    totals_out,
    norm_mine,
    norm_all,
    norm_plane,
    norm_line,
    core_send,
    core_recv,
    plane_send,
    plane_all,
    line_send,
    line_all,
    ext_core_send,
    ext_core_recv,
    ext_plane_send,
    ext_plane_all,
    ext_line_send,
    ext_line_all,
    load_sems,
    store_sems,
    norm_sems,
    norm_line_sems,
    halo_send_sems,
    halo_recv_sems,
    core_sems,
    plane_send_sems,
    plane_recv_sems,
    line_send_sems,
    line_recv_sems,
    ext_core_sems,
    ext_plane_send_sems,
    ext_plane_recv_sems,
    ext_line_send_sems,
    ext_line_recv_sems,
    spread_send_sems,
    spread_recv_sems,
    pair_send_sems,
    pair_recv_sems,
):
    gx, gz = dims
    channels, x_elems, z_elems, line = state_ref.shape
    hidden = w_mid_ref.shape[0]
    columns = x_elems * z_elems
    count = gx * gz
    half = hidden // 2
    n_plane, n_line = gx * 2, gz // 4
    part = hidden // n_plane
    nodes = inv_ref.shape[0]
    pieces = 4
    piece = nodes // pieces
    my_x, my_z = lax.axis_index("gx"), lax.axis_index("gz")
    me = my_x * gz + my_z
    core, side, level = my_z % 2, (my_z // 2) % 2, my_z // 4
    my_plane = my_x * 2 + side
    other_core = (my_x, my_z + 1 - 2 * core)

    loads = [
        pltpu.make_async_copy(src, dst, load_sems.at[spot])
        for spot, (src, dst) in enumerate(
            (
                (state_hbm, state_ref),
                (cot_hbm, cot_ref),
                (w_in_hbm, w_in_ref),
                (b_in_hbm, b_in_ref),
                (w_mid_hbm, w_mid_ref),
                (b_mid_hbm, b_mid_ref),
                (tags_hbm, tags_ref),
            )
        )
    ]
    inv_loads = [
        pltpu.make_async_copy(
            inv_hbm.at[pl.ds(p * piece, piece)],
            inv_ref.at[pl.ds(p * piece, piece)],
            load_sems.at[len(loads) + p],
        )
        for p in range(pieces)
    ]
    for load in loads[2:] + loads[:2] + inv_loads:
        load.start()

    barrier = pltpu.get_barrier_semaphore()

    def plane_peer(d):
        to = lax.rem(my_plane + d, n_plane)
        return to, (to // 2, level * 4 + lax.rem(to, 2) * 2 + core)

    def line_peer(d):
        return (my_x, lax.rem(level + d, n_line) * 4 + side * 2 + core)

    def next_x(d):
        return (lax.rem(my_x + gx + d, gx), my_z)

    def next_z(d):
        return (my_x, lax.rem(my_z + gz + d, gz))

    plane_peers = [other_core]
    for d in range(1, n_plane):
        x, z = plane_peer(d)[1]
        plane_peers += [(x, z), (x, z + 1 - 2 * core)]
    line_peers = [line_peer(d) for d in range(1, n_line)]
    friends = plane_peers + line_peers + [next_z(-1), next_z(1)]
    for friend in friends:
        pl.semaphore_signal(barrier, inc=1, device_id=friend, device_id_type=MESH)

    loads[0].wait()
    squares = state_ref[...] * state_ref[...]
    squares = jnp.sum(jnp.sum(squares, axis=0), axis=0)
    folded = squares[:, :128]
    for start in range(128, line, 128):
        folded = folded + squares[:, start : start + 128]
    norm_mine[...] = jnp.sum(folded, axis=0, keepdims=True)

    pl.semaphore_wait(barrier, len(friends))

    def send_norm(source, slots, sems, peers):
        for spot, peer in enumerate(peers):
            pltpu.make_async_remote_copy(
                src_ref=source,
                dst_ref=slots.at[spot],
                send_sem=sems.at[0],
                recv_sem=sems.at[1],
                device_id=peer,
                device_id_type=MESH,
            ).start()

    def wait_norm(slots, sems, size):
        whole = slots.at[pl.ds(0, size)]
        pltpu.make_async_copy(whole, whole, sems.at[0]).wait()
        pltpu.make_async_copy(whole, whole, sems.at[1]).wait()
        return jnp.sum(slots[0:size], axis=0)

    send_norm(norm_mine, norm_all, norm_sems, plane_peers)

    for load in loads[2:]:
        load.wait()
    w_in = w_in_ref[...]
    w_high = rounded(w_in)
    w_low = rounded(w_in - w_high)
    b_in = b_in_ref[...]
    b_high = rounded(b_in)
    b_next = rounded(b_in - b_high)
    b_last = rounded(b_in - b_high - b_next)
    joint_rows = jnp.concatenate(
        [w_high, b_high, b_next, b_last, w_high, jnp.zeros((8 - channels, hidden), F32)]
        + [w_low, jnp.zeros((16 - channels, hidden), F32)],
        axis=0,
    )
    w_first[...] = (0.5 * joint_rows).T.astype(BF16)
    w_back[...] = joint_rows[8:24].astype(BF16)
    w_mid = 0.5 * w_mid_ref[...].astype(F32)
    w_mid_half[...] = w_mid.astype(BF16)
    w_mid_t[...] = w_mid.T.astype(BF16)
    w_out_half[...] = jnp.concatenate(
        [0.5 * w_out_ref[...].astype(F32), jnp.zeros((16 - channels, hidden), F32)], axis=0
    ).T.astype(BF16)
    bias = jnp.broadcast_to(0.5 * b_mid_ref[...], (128, hidden)).T
    bias_mid[...] = bias
    totals[...] = jnp.zeros_like(totals)
    totals_in[...] = jnp.zeros_like(totals_in)
    totals_out[...] = jnp.zeros_like(totals_out)

    loads[1].wait()
    for c in range(channels):
        for i in range(x_elems):
            low_x[c, i * z_elems : (i + 1) * z_elems, :] = cot_ref[c, i]
    lane = lax.broadcasted_iota(jnp.int32, (columns, 128), 1)
    first_lane = lane & 64
    blocks = line // 128

    def adjoint_step(n, sums):
        spot = first_lane + n
        rows = jnp.concatenate([inv_ref[n, i] for i in range(x_elems)], axis=0)
        out = []
        for c in range(channels):
            for t in range(blocks):
                tile = low_x[c, :, t * 128 : (t + 1) * 128]
                spread = jnp.take_along_axis(tile, spot, axis=1)
                out.append(
                    sums[c * blocks + t] + rows[:, t * 128 : (t + 1) * 128] * spread
                )
        return tuple(out)

    sums = (jnp.zeros((columns, 128), F32),) * (channels * blocks)
    for p in range(pieces):
        inv_loads[p].wait()
        sums = lax.fori_loop(p * piece, (p + 1) * piece, adjoint_step, sums, unroll=piece)
        if p == 1:
            norm_plane[...] = norm_mine[...] + wait_norm(norm_all, norm_sems, len(plane_peers))
            send_norm(norm_plane, norm_line, norm_line_sems, line_peers)
    for c in range(channels):
        for t in range(blocks):
            adj_rows[c, :, t * 128 : (t + 1) * 128] = sums[c * blocks + t]

    for c in range(channels):
        x_send[0, c] = adj_rows[c, 0:z_elems, :]
        x_send[1, c] = adj_rows[c, columns - z_elems : columns, :]
        for i in range(x_elems):
            z_send[0, c * x_elems + i] = adj_rows[c, i * z_elems : i * z_elems + 1, :]
            z_send[1, c * x_elems + i] = adj_rows[
                c, (i + 1) * z_elems - 1 : (i + 1) * z_elems, :
            ]
    halo_copies = []
    for spot, (src, dst, to) in enumerate(
        (
            (x_send.at[0], x_halo.at[1], next_x(-1)),
            (x_send.at[1], x_halo.at[0], next_x(1)),
            (z_send.at[0], z_halo.at[1], next_z(-1)),
            (z_send.at[1], z_halo.at[0], next_z(1)),
        )
    ):
        copy = pltpu.make_async_remote_copy(
            src_ref=src,
            dst_ref=dst,
            send_sem=halo_send_sems.at[spot],
            recv_sem=halo_recv_sems.at[spot],
            device_id=to,
            device_id_type=MESH,
        )
        copy.start()
        halo_copies.append(copy)

    for i in range(x_elems):
        for k in range(z_elems):
            row = i * z_elems + k
            state_rows[row] = jnp.ones((8, line), F32)
            grad_rows[row] = jnp.zeros((16, line), F32)
            for c in range(channels):
                state_rows[row, c : c + 1, :] = state_ref[c, i, k : k + 1, :]
                grad_rows[row, c : c + 1, :] = DT_STEP * adj_rows[c, row : row + 1, :]
    sum_squares = norm_plane[...]
    if line_peers:
        sum_squares = sum_squares + wait_norm(norm_line, norm_line_sems, len(line_peers))
    sum_squares = jnp.sum(sum_squares, axis=1, keepdims=True)
    entry_count = channels * columns * line * count
    inv_norm = lax.rsqrt(sum_squares / entry_count + EPS)
    row_index = lax.broadcasted_iota(jnp.int32, (8, line), 0)
    scale = jnp.where(row_index < channels, jnp.broadcast_to(inv_norm, (8, line)), 1.0)

    def first_layer(row):
        scaled = state_rows[row] * scale
        high = rounded(scaled)
        low = scaled - high
        inputs = jnp.concatenate([high, low, high, jnp.zeros_like(high)], axis=0).astype(BF16)
        joints[row, hidden:, :] = inputs
        pre = nn_dot(w_first[...], inputs)
        bend = jnp.tanh(pre)
        gate = 1.0 + bend
        act = pre * gate
        bends[row] = bend
        joints[row, :hidden, :] = act.astype(BF16)

    def second_layer(row):
        pre = nn_dot(w_mid_t[...], joints[row, :hidden, :])
        pre = pre + jnp.concatenate([bias_mid[...]] * (line // 128), axis=1)
        bend = jnp.tanh(pre)
        gate = 1.0 + bend
        act = pre * gate
        slope_two = gate + act * (1.0 - bend)
        out_grad = grad_rows[row].astype(BF16)
        hiddens[row] = act.astype(BF16)
        back_two = nn_dot(w_out_half[...], out_grad)
        deltas[row] = (back_two * slope_two).astype(BF16)

    def last_layer(row):
        totals[...] += nt_dot(joints[row], deltas[row])

    for step in range(columns + 2):
        if step < columns:
            first_layer(step)
        if 1 <= step <= columns:
            second_layer(step - 1)
        if step >= 2:
            last_layer(step - 2)

    def backward(row):
        bend = bends[row]
        slope = 1.0 + bend + joints[row, :hidden, :].astype(F32) * (1.0 - bend)
        delta_one = nn_dot(w_mid_half[...], deltas[row]) * slope
        delta_one = delta_one.astype(BF16)
        totals_in[...] += nt_dot(joints[row, hidden:, :], delta_one)
        totals_out[...] += nt_dot(grad_rows[row].astype(BF16), hiddens[row])
        back = nn_dot(w_back[...], delta_one)
        back = back[:8] + back[8:]
        for c in range(channels):
            back_rows[c, row : row + 1, :] = back[c : c + 1, :]

    def remote(src, dst, send_sem, recv_sem, to):
        copy = pltpu.make_async_remote_copy(
            src_ref=src,
            dst_ref=dst,
            send_sem=send_sem,
            recv_sem=recv_sem,
            device_id=to,
            device_id_type=MESH,
        )
        copy.start()
        return copy

    def ordered_sum(ref, size):
        return sum((ref[q] for q in range(1, size)), ref[0])

    for h in range(2):
        core_send[h] = totals[0:hidden, h * half : (h + 1) * half]
    core_copy = remote(
        core_send.at[1 - core], core_recv, core_sems.at[0], core_sems.at[1], other_core
    )
    early, middle = 3 * columns // 8, 6 * columns // 8
    for row in range(early):
        backward(row)

    core_copy.wait()
    for q in range(n_plane):
        rows = slice(q * part, (q + 1) * part)
        plane_send[q] = core_send[core, rows, :] + core_recv[rows, :]
    plane_copies = []
    for d in range(1, n_plane):
        to, device = plane_peer(d)
        plane_copies.append(
            remote(
                plane_send.at[to],
                plane_all.at[my_plane],
                plane_send_sems.at[d],
                plane_recv_sems.at[d],
                device,
            )
        )
    plane_all[my_plane] = plane_send[my_plane]
    for row in range(early, middle):
        backward(row)

    for copy in plane_copies:
        copy.wait()
    line_send[...] = ordered_sum(plane_all, n_plane)
    line_copies = [
        remote(
            line_send,
            line_all.at[level],
            line_send_sems.at[d],
            line_recv_sems.at[d],
            line_peer(d),
        )
        for d in range(1, n_line)
    ]
    line_all[level] = line_send[...]

    for row in range(middle, columns):
        backward(row)
    top = lax.broadcasted_iota(jnp.int32, (8, hidden), 0)
    mixed = jnp.where(
        top == channels + 1, totals[hidden : hidden + 8], totals_in[0:8] + totals_in[8:16]
    )
    for h in range(2):
        lanes = slice(h * half, (h + 1) * half)
        ext_core_send[h, 0:8, :] = mixed[:, lanes]
        ext_core_send[h, 8:16, :] = totals_out[0:8, lanes]
    ext_core_copy = remote(
        ext_core_send.at[1 - core],
        ext_core_recv,
        ext_core_sems.at[0],
        ext_core_sems.at[1],
        other_core,
    )

    ext_plane_copies = []

    def start_ext_plane():
        ext_core_copy.wait()
        ext_plane_send[...] = ext_core_send[core] + ext_core_recv[...]
        ext_plane_copies.extend(
            remote(
                ext_plane_send,
                ext_plane_all.at[my_plane],
                ext_plane_send_sems.at[d],
                ext_plane_recv_sems.at[d],
                plane_peer(d)[1],
            )
            for d in range(1, n_plane)
        )
        ext_plane_all[my_plane] = ext_plane_send[...]

    for copy in halo_copies:
        copy.wait()
    for c in range(channels):
        low_x[c, 0:z_elems, :] = x_halo[0, c]
        up_x[c, columns - z_elems : columns, :] = x_halo[1, c]
        if x_elems > 1:
            low_x[c, z_elems:columns, :] = adj_rows[c, 0 : columns - z_elems, :]
            up_x[c, 0 : columns - z_elems, :] = adj_rows[c, z_elems:columns, :]
        for i in range(x_elems):
            first, last = i * z_elems, (i + 1) * z_elems
            low_z[c, first : first + 1, :] = z_halo[0, c * x_elems + i]
            up_z[c, last - 1 : last, :] = z_halo[1, c * x_elems + i]
            if z_elems > 1:
                low_z[c, first + 1 : last, :] = adj_rows[c, first : last - 1, :]
                up_z[c, first : last - 1, :] = adj_rows[c, first + 1 : last, :]
    lane = lax.broadcasted_iota(jnp.int32, (columns, line), 1)
    row = lax.broadcasted_iota(jnp.int32, (columns, line), 0)
    spot_a, spot_b, spot_c, spot_j = (lane >> 4) & 3, (lane >> 2) & 3, lane & 3, lane >> 6
    bottom = jnp.zeros((columns, line), F32)
    ceiling = jnp.zeros((columns, line), F32)
    for i in range(x_elems):
        for k in range(z_elems):
            here = row == i * z_elems + k
            bottom = jnp.where(here, -2.0 * tags_ref[0, i, k].astype(F32), bottom)
            ceiling = jnp.where(here, -2.0 * tags_ref[1, i, k].astype(F32), ceiling)
    for c in range(channels):
        if c == channels // 2:
            start_ext_plane()
        own = adj_rows[c]
        low_y = jnp.where(spot_j == 0, bottom * own, pltpu.roll(own, 52, 1) - own)
        up_y = jnp.where(
            spot_j == line // 64 - 1, ceiling * own, pltpu.roll(own, line - 52, 1) - own
        )
        jump = (
            jnp.where(spot_a == 0, pltpu.roll(low_x[c], line - 48, 1) - own, 0.0)
            + jnp.where(spot_a == 3, pltpu.roll(up_x[c], 48, 1) - own, 0.0)
            + jnp.where(spot_b == 0, low_y, 0.0)
            + jnp.where(spot_b == 3, up_y, 0.0)
            + jnp.where(spot_c == 0, pltpu.roll(low_z[c], line - 3, 1) - own, 0.0)
            + jnp.where(spot_c == 3, pltpu.roll(up_z[c], 3, 1) - own, 0.0)
        )
        back_rows[c] = own + 0.5 * KAPPA * jump + inv_norm * back_rows[c]
        for i in range(x_elems):
            gstate_ref[c, i] = back_rows[c, i * z_elems : (i + 1) * z_elems, :]
    stores = []

    def store(src, dst):
        copy = pltpu.make_async_copy(src, dst, store_sems.at[len(stores)])
        copy.start()
        stores.append(copy)

    def store_part(h, q):
        dst = gmid_hbm.at[
            pl.ds(pl.multiple_of(q * part, part), part),
            pl.ds(pl.multiple_of(h * half, half), half),
        ]
        store(gathered.at[h, q], dst)

    store(gstate_ref, gstate_hbm)

    for copy in ext_plane_copies:
        copy.wait()
    ext_line_send[...] = ordered_sum(ext_plane_all, n_plane)
    ext_line_copies = [
        remote(
            ext_line_send,
            ext_line_all.at[level],
            ext_line_send_sems.at[d],
            ext_line_recv_sems.at[d],
            line_peer(d),
        )
        for d in range(1, n_line)
    ]
    ext_line_all[level] = ext_line_send[...]

    def to_pair(slot, d):
        return remote(
            gathered.at[core, slot],
            gathered.at[core, slot],
            pair_send_sems.at[d],
            pair_recv_sems.at[d],
            other_core,
        )

    factor = 4.0 / math.sqrt(entry_count // channels)
    for copy in line_copies:
        copy.wait()
    gathered[core, my_plane] = factor * ordered_sum(line_all, n_line)
    spread_copies = [
        remote(
            gathered.at[core, my_plane],
            gathered.at[core, my_plane],
            spread_send_sems.at[d],
            spread_recv_sems.at[d],
            plane_peer(d)[1],
        )
        for d in range(1, n_plane)
    ]
    pair_copies = [to_pair(my_plane, 0)]
    store_part(core, my_plane)
    for d in range(1, n_plane):
        spread_copies[d - 1].wait_recv()
        slot = lax.rem(my_plane + n_plane - d, n_plane)
        pair_copies.append(to_pair(slot, d))
        store_part(core, slot)
    for copy in ext_line_copies:
        copy.wait()
    gathered_ext[core] = factor * ordered_sum(ext_line_all, n_line)
    ext_pair_copy = remote(
        gathered_ext.at[core],
        gathered_ext.at[core],
        pair_send_sems.at[n_plane],
        pair_recv_sems.at[n_plane],
        other_core,
    )
    ext_pair_copy.wait()
    for h in range(2):
        lanes = slice(h * half, (h + 1) * half)
        gin_ref[:, lanes] = gathered_ext[h, 0:channels]
        gbin_ref[:, lanes] = gathered_ext[h, channels : channels + 1]
        gbmid_ref[:, lanes] = gathered_ext[h, channels + 1 : channels + 2]
        gout_ref[:, lanes] = gathered_ext[h, 8 : 8 + channels]
    store(gin_ref, gin_hbm)
    store(gbin_ref, gbin_hbm)
    store(gbmid_ref, gbmid_hbm)
    store(gout_ref, gout_hbm)
    for d in range(n_plane):
        pair_copies[d].wait()
        store_part(1 - core, lax.rem(my_plane + n_plane - d, n_plane))
    for copy in spread_copies:
        copy.wait_send()
    for copy in stores:
        copy.wait()


def writer(*refs):
    size = (len(refs) - 1) // 3
    sems = refs[-1]
    sources, results, held = refs[:size], refs[size : 2 * size], refs[2 * size : -1]
    loads = [
        pltpu.make_async_copy(sources[spot], held[spot], sems.at[spot]) for spot in range(size)
    ]
    stores = [
        pltpu.make_async_copy(held[spot], results[spot], sems.at[size + spot])
        for spot in range(size)
    ]
    for load in loads:
        load.start()
    for load, store in zip(loads, stores):
        load.wait()
        store.start()
    for store in stores:
        store.wait()


def per_device(dims, state, cotangent, local_inverse, wall_tags, w_in, b_in, w_mid, b_mid, w_out):
    gx, gz = dims
    channels, x_elems, z_elems, line = state.shape
    hidden = w_mid.shape[0]
    columns = x_elems * z_elems
    n_plane, n_line = gx * 2, gz // 4
    part = hidden // n_plane
    half = hidden // 2
    vmem = pl.BlockSpec(memory_space=pltpu.VMEM)
    hbm = pl.BlockSpec(memory_space=pltpu.HBM)
    rows = pltpu.VMEM((channels, columns, line), F32)
    dma = pltpu.SemaphoreType.DMA

    def same(array):
        return pltpu.VMEM(array.shape, array.dtype)

    b_in, b_mid = b_in.reshape(1, hidden), b_mid.reshape(1, hidden)
    out_shape = (
        jax.ShapeDtypeStruct(state.shape, F32),
        jax.ShapeDtypeStruct((channels, hidden), F32),
        jax.ShapeDtypeStruct((1, hidden), F32),
        jax.ShapeDtypeStruct((hidden, hidden), F32),
        jax.ShapeDtypeStruct((1, hidden), F32),
        jax.ShapeDtypeStruct((channels, hidden), F32),
    )
    out = pl.pallas_call(
        functools.partial(kernel, dims),
        out_shape=out_shape,
        in_specs=[hbm] * 8 + [vmem],
        out_specs=(hbm,) * 6,
        scratch_shapes=[
            same(state),
            pltpu.VMEM((channels, hidden), F32),
            pltpu.VMEM((1, hidden), F32),
            pltpu.VMEM((1, hidden), F32),
            pltpu.VMEM((channels, hidden), F32),
            pltpu.VMEM((2, n_plane, part, half), F32),
            pltpu.VMEM((2, 16, half), F32),
            same(state),
            same(cotangent),
            same(local_inverse),
            pltpu.SMEM(wall_tags.shape, jnp.int32),
            same(w_in),
            same(b_in),
            same(w_mid),
            same(b_mid),
            pltpu.VMEM((columns, 8, line), F32),
            pltpu.VMEM((columns, 16, line), F32),
            rows,
            rows,
            rows,
            rows,
            rows,
            rows,
            pltpu.VMEM((2, channels, z_elems, line), F32),
            pltpu.VMEM((2, channels, z_elems, line), F32),
            pltpu.VMEM((2, channels * x_elems, 1, line), F32),
            pltpu.VMEM((2, channels * x_elems, 1, line), F32),
            pltpu.VMEM((hidden, 32), BF16),
            pltpu.VMEM((16, hidden), BF16),
            pltpu.VMEM((hidden, hidden), BF16),
            pltpu.VMEM((hidden, hidden), BF16),
            pltpu.VMEM((hidden, 16), BF16),
            pltpu.VMEM((hidden, 128), F32),
            pltpu.VMEM((columns, hidden + 32, line), BF16),
            pltpu.VMEM((columns, hidden, line), F32),
            pltpu.VMEM((columns, hidden, line), BF16),
            pltpu.VMEM((columns, hidden, line), BF16),
            pltpu.VMEM((hidden + 32, hidden), F32),
            pltpu.VMEM((32, hidden), F32),
            pltpu.VMEM((16, hidden), F32),
            pltpu.VMEM((1, 128), F32),
            pltpu.VMEM((2 * n_plane, 1, 128), F32),
            pltpu.VMEM((1, 128), F32),
            pltpu.VMEM((n_line, 1, 128), F32),
            pltpu.VMEM((2, hidden, half), F32),
            pltpu.VMEM((hidden, half), F32),
            pltpu.VMEM((n_plane, part, half), F32),
            pltpu.VMEM((n_plane, part, half), F32),
            pltpu.VMEM((part, half), F32),
            pltpu.VMEM((n_line, part, half), F32),
            pltpu.VMEM((2, 16, half), F32),
            pltpu.VMEM((16, half), F32),
            pltpu.VMEM((16, half), F32),
            pltpu.VMEM((n_plane, 16, half), F32),
            pltpu.VMEM((16, half), F32),
            pltpu.VMEM((n_line, 16, half), F32),
            dma((11,)),
            dma((2 * n_plane + 5,)),
            dma((2,)),
            dma((2,)),
            dma((4,)),
            dma((4,)),
            dma((2,)),
            dma((n_plane,)),
            dma((n_plane,)),
            dma((n_line,)),
            dma((n_line,)),
            dma((2,)),
            dma((n_plane,)),
            dma((n_plane,)),
            dma((n_line,)),
            dma((n_line,)),
            dma((n_plane,)),
            dma((n_plane,)),
            dma((n_plane + 1,)),
            dma((n_plane + 1,)),
        ],
        compiler_params=pltpu.CompilerParams(
            collective_id=0, has_side_effects=True, vmem_limit_bytes=62 * 1024 * 1024
        ),
    )(state, cotangent, local_inverse, wall_tags, w_in, b_in, w_mid, b_mid, w_out.T)
    out = pl.pallas_call(
        writer,
        out_shape=out_shape,
        in_specs=[hbm] * 6,
        out_specs=(hbm,) * 6,
        scratch_shapes=[pltpu.VMEM(o.shape, F32) for o in out_shape] + [dma((12,))],
        compiler_params=pltpu.CompilerParams(vmem_limit_bytes=62 * 1024 * 1024),
    )(*out)
    return out[0], out[1], out[2].reshape(hidden), out[3], out[4].reshape(hidden), out[5].T


def solution(mesh):
    placed = (
        P(None, "gx", "gz", None),
        P(None, "gx", "gz", None),
        P(None, "gx", "gz", None),
        P(None, "gx", "gz"),
        P(),
        P(),
        P(),
        P(),
        P(),
    )
    return jax.shard_map(
        functools.partial(per_device, (mesh.shape["gx"], mesh.shape["gz"])),
        mesh=mesh,
        in_specs=placed,
        out_specs=(P(None, "gx", "gz", None), P(), P(), P(), P(), P()),
        check_vma=False,
    )
```

```python
import functools
import math

import jax
import jax.numpy as jnp
from jax import lax
from jax.experimental import pallas as pl
from jax.experimental.pallas import tpu as pltpu
from jax.sharding import PartitionSpec as P

KAPPA = 0.5
DT_STEP = 0.5
EPS = 1e-06
F32 = jnp.float32
BF16 = jnp.bfloat16
MESH = pl.DeviceIdType.MESH


def nt_dot(first_op, second_op):
    return lax.dot_general(
        first_op, second_op, (((1,), (1,)), ((), ())), preferred_element_type=F32
    )


def nn_dot(first_op, second_op):
    return jnp.dot(first_op, second_op, preferred_element_type=F32)


def rounded(value):
    return value.astype(BF16).astype(F32)


def kernel(
    dims,
    state_hbm,
    cot_hbm,
    inv_hbm,
    tags_hbm,
    w_in_hbm,
    b_in_hbm,
    w_mid_hbm,
    b_mid_hbm,
    w_out_ref,
    gstate_hbm,
    gin_hbm,
    gbin_hbm,
    gmid_hbm,
    gbmid_hbm,
    gout_hbm,
    gstate_ref,
    gin_ref,
    gbin_ref,
    gbmid_ref,
    gout_ref,
    state_ref,
    cot_ref,
    inv_ref,
    tags_ref,
    w_in_ref,
    b_in_ref,
    w_mid_ref,
    b_mid_ref,
    state_rows,
    grad_rows,
    adj_rows,
    back_rows,
    low_x,
    up_x,
    low_z,
    up_z,
    x_send,
    x_halo,
    z_send,
    z_halo,
    w_first,
    w_back,
    w_mid_t,
    w_mid_half,
    w_out_half,
    bias_mid,
    joints,
    bends,
    hiddens,
    deltas,
    totals,
    totals_in,
    totals_out,
    norm_mine,
    norm_all,
    plane_all,
    line_send,
    line_all,
    result,
    ext_send,
    ext_plane_all,
    ext_line_send,
    ext_line_all,
    load_sems,
    store_sems,
    norm_sems,
    halo_send_sems,
    halo_recv_sems,
    plane_send_sems,
    plane_recv_sems,
    line_send_sems,
    line_recv_sems,
    ext_plane_send_sems,
    ext_plane_recv_sems,
    ext_line_send_sems,
    ext_line_recv_sems,
    spread_send_sems,
    spread_recv_sems,
):
    gx, gz = dims
    channels, x_elems, z_elems, line = state_ref.shape
    hidden = w_mid_ref.shape[0]
    columns = x_elems * z_elems
    count = gx * gz
    n_plane, n_line = gx * 4, gz // 4
    part = hidden // n_plane
    halves, _, span, _ = plane_all.shape
    nodes = inv_ref.shape[0]
    pieces = 4
    piece = nodes // pieces
    my_x, my_z = lax.axis_index("gx"), lax.axis_index("gz")
    me = my_x * gz + my_z
    spot_z, level = my_z % 4, my_z // 4
    mine = my_x * 4 + spot_z

    loads = [
        pltpu.make_async_copy(src, dst, load_sems.at[spot])
        for spot, (src, dst) in enumerate(
            (
                (state_hbm, state_ref),
                (cot_hbm, cot_ref),
                (w_in_hbm, w_in_ref),
                (b_in_hbm, b_in_ref),
                (w_mid_hbm, w_mid_ref),
                (b_mid_hbm, b_mid_ref),
                (tags_hbm, tags_ref),
            )
        )
    ]
    inv_loads = [
        pltpu.make_async_copy(
            inv_hbm.at[pl.ds(p * piece, piece)],
            inv_ref.at[pl.ds(p * piece, piece)],
            load_sems.at[len(loads) + p],
        )
        for p in range(pieces)
    ]
    for load in loads[2:] + loads[:2] + inv_loads:
        load.start()

    barrier = pltpu.get_barrier_semaphore()

    def greet(step, carry):
        to = lax.rem(me + step, count)
        pl.semaphore_signal(
            barrier, inc=1, device_id=(to // gz, lax.rem(to, gz)), device_id_type=MESH
        )
        return carry

    lax.fori_loop(1, count, greet, 0)

    loads[0].wait()
    squares = state_ref[...] * state_ref[...]
    squares = jnp.sum(jnp.sum(squares, axis=0), axis=0)
    folded = squares[:, :128]
    for start in range(128, line, 128):
        folded = folded + squares[:, start : start + 128]
    norm_mine[...] = jnp.sum(folded, axis=0, keepdims=True)

    pl.semaphore_wait(barrier, count - 1)

    def send_norm(step, carry):
        to = lax.rem(me + step, count)
        pltpu.make_async_remote_copy(
            src_ref=norm_mine,
            dst_ref=norm_all.at[step - 1],
            send_sem=norm_sems.at[0],
            recv_sem=norm_sems.at[1],
            device_id=(to // gz, lax.rem(to, gz)),
            device_id_type=MESH,
        ).start()
        return carry

    lax.fori_loop(1, count, send_norm, 0)

    for load in loads[2:]:
        load.wait()
    w_in = w_in_ref[...]
    w_high = rounded(w_in)
    w_low = rounded(w_in - w_high)
    b_in = b_in_ref[...]
    b_high = rounded(b_in)
    b_next = rounded(b_in - b_high)
    b_last = rounded(b_in - b_high - b_next)
    joint_rows = jnp.concatenate(
        [w_high, b_high, b_next, b_last, w_high, jnp.zeros((8 - channels, hidden), F32)]
        + [w_low, jnp.zeros((16 - channels, hidden), F32)],
        axis=0,
    )
    w_first[...] = (0.5 * joint_rows).T.astype(BF16)
    w_back[...] = joint_rows[8:24].astype(BF16)
    w_mid = 0.5 * w_mid_ref[...].astype(F32)
    w_mid_half[...] = w_mid.astype(BF16)
    w_mid_t[...] = w_mid.T.astype(BF16)
    w_out_half[...] = jnp.concatenate(
        [0.5 * w_out_ref[...].astype(F32), jnp.zeros((16 - channels, hidden), F32)], axis=0
    ).T.astype(BF16)
    bias = jnp.broadcast_to(0.5 * b_mid_ref[...], (128, hidden)).T
    bias_mid[...] = bias
    totals[...] = jnp.zeros_like(totals)
    totals_in[...] = jnp.zeros_like(totals_in)
    totals_out[...] = jnp.zeros_like(totals_out)

    loads[1].wait()
    for c in range(channels):
        for i in range(x_elems):
            low_x[c, i * z_elems : (i + 1) * z_elems, :] = cot_ref[c, i]
    lane = lax.broadcasted_iota(jnp.int32, (columns, 128), 1)
    first_lane = lane & 64
    blocks = line // 128

    def adjoint_step(n, sums):
        spot = first_lane + n
        rows = jnp.concatenate([inv_ref[n, i] for i in range(x_elems)], axis=0)
        out = []
        for c in range(channels):
            for t in range(blocks):
                tile = low_x[c, :, t * 128 : (t + 1) * 128]
                spread = jnp.take_along_axis(tile, spot, axis=1)
                out.append(
                    sums[c * blocks + t] + rows[:, t * 128 : (t + 1) * 128] * spread
                )
        return tuple(out)

    sums = (jnp.zeros((columns, 128), F32),) * (channels * blocks)
    for p in range(pieces):
        inv_loads[p].wait()
        sums = lax.fori_loop(p * piece, (p + 1) * piece, adjoint_step, sums, unroll=piece)
    for c in range(channels):
        for t in range(blocks):
            adj_rows[c, :, t * 128 : (t + 1) * 128] = sums[c * blocks + t]

    for c in range(channels):
        x_send[0, c] = adj_rows[c, 0:z_elems, :]
        x_send[1, c] = adj_rows[c, columns - z_elems : columns, :]
        for i in range(x_elems):
            z_send[0, c * x_elems + i] = adj_rows[c, i * z_elems : i * z_elems + 1, :]
            z_send[1, c * x_elems + i] = adj_rows[
                c, (i + 1) * z_elems - 1 : (i + 1) * z_elems, :
            ]
    halo_copies = []
    for spot, (src, dst, to) in enumerate(
        (
            (x_send.at[0], x_halo.at[1], (lax.rem(my_x + gx - 1, gx), my_z)),
            (x_send.at[1], x_halo.at[0], (lax.rem(my_x + 1, gx), my_z)),
            (z_send.at[0], z_halo.at[1], (my_x, lax.rem(my_z + gz - 1, gz))),
            (z_send.at[1], z_halo.at[0], (my_x, lax.rem(my_z + 1, gz))),
        )
    ):
        copy = pltpu.make_async_remote_copy(
            src_ref=src,
            dst_ref=dst,
            send_sem=halo_send_sems.at[spot],
            recv_sem=halo_recv_sems.at[spot],
            device_id=to,
            device_id_type=MESH,
        )
        copy.start()
        halo_copies.append(copy)

    for i in range(x_elems):
        for k in range(z_elems):
            row = i * z_elems + k
            state_rows[row] = jnp.ones((8, line), F32)
            grad_rows[row] = jnp.zeros((16, line), F32)
            for c in range(channels):
                state_rows[row, c : c + 1, :] = state_ref[c, i, k : k + 1, :]
                grad_rows[row, c : c + 1, :] = DT_STEP * adj_rows[c, row : row + 1, :]
    whole = norm_all.at[pl.ds(0, count - 1)]
    pltpu.make_async_copy(whole, whole, norm_sems.at[0]).wait()
    pltpu.make_async_copy(whole, whole, norm_sems.at[1]).wait()
    sum_squares = norm_mine[...] + jnp.sum(norm_all[0 : count - 1], axis=0)
    sum_squares = jnp.sum(sum_squares, axis=1, keepdims=True)
    entry_count = channels * columns * line * count
    inv_norm = lax.rsqrt(sum_squares / entry_count + EPS)
    row_index = lax.broadcasted_iota(jnp.int32, (8, line), 0)
    scale = jnp.where(row_index < channels, jnp.broadcast_to(inv_norm, (8, line)), 1.0)

    def first_layer(row):
        scaled = state_rows[row] * scale
        high = rounded(scaled)
        low = scaled - high
        inputs = jnp.concatenate([high, low, high, jnp.zeros_like(high)], axis=0).astype(BF16)
        joints[row, hidden:, :] = inputs
        pre = nn_dot(w_first[...], inputs)
        bend = jnp.tanh(pre)
        gate = 1.0 + bend
        act = pre * gate
        bends[row] = bend
        joints[row, :hidden, :] = act.astype(BF16)

    def second_layer(row):
        pre = nn_dot(w_mid_t[...], joints[row, :hidden, :])
        pre = pre + jnp.concatenate([bias_mid[...]] * (line // 128), axis=1)
        bend = jnp.tanh(pre)
        gate = 1.0 + bend
        act = pre * gate
        slope_two = gate + act * (1.0 - bend)
        out_grad = grad_rows[row].astype(BF16)
        hiddens[row] = act.astype(BF16)
        back_two = nn_dot(w_out_half[...], out_grad)
        deltas[row] = (back_two * slope_two).astype(BF16)

    def last_layer(row):
        totals[...] += nt_dot(joints[row], deltas[row])

    for step in range(columns + 2):
        if step < columns:
            first_layer(step)
        if 1 <= step <= columns:
            second_layer(step - 1)
        if step >= 2:
            last_layer(step - 2)

    def backward(row):
        bend = bends[row]
        slope = 1.0 + bend + joints[row, :hidden, :].astype(F32) * (1.0 - bend)
        delta_one = nn_dot(w_mid_half[...], deltas[row]) * slope
        delta_one = delta_one.astype(BF16)
        totals_in[...] += nt_dot(joints[row, hidden:, :], delta_one)
        totals_out[...] += nt_dot(grad_rows[row].astype(BF16), hiddens[row])
        back = nn_dot(w_back[...], delta_one)
        back = back[:8] + back[8:]
        for c in range(channels):
            back_rows[c, row : row + 1, :] = back[c : c + 1, :]

    def remote(src, dst, send_sem, recv_sem, to):
        copy = pltpu.make_async_remote_copy(
            src_ref=src,
            dst_ref=dst,
            send_sem=send_sem,
            recv_sem=recv_sem,
            device_id=to,
            device_id_type=MESH,
        )
        copy.start()
        return copy

    def plane_peer(d):
        to = lax.rem(mine + d, n_plane)
        return to, (to // 4, level * 4 + lax.rem(to, 4))

    def line_peer(d):
        return (my_x, lax.rem(level + d, n_line) * 4 + spot_z)

    def ordered_sum(ref, size):
        return sum((ref[q] for q in range(1, size)), ref[0])

    def wait_all(copies):
        for copy in copies:
            copy.wait()

    def block_of(owner, t):
        return pl.ds(pl.multiple_of(owner * part + t * span, span), span)

    plane_copies = []
    for t in range(halves):
        copies = []
        for d in range(1, n_plane):
            to, device = plane_peer(d)
            copies.append(
                remote(
                    totals.at[block_of(to, t)],
                    plane_all.at[t, mine],
                    plane_send_sems.at[t, d],
                    plane_recv_sems.at[t, d],
                    device,
                )
            )
        plane_copies.append(copies)
        plane_all[t, mine] = totals[block_of(mine, t), :]

    line_copies = []

    def start_line(t):
        wait_all(plane_copies[t])
        line_send[t] = ordered_sum(plane_all.at[t], n_plane)
        line_copies.append(
            [
                remote(
                    line_send.at[t],
                    line_all.at[t, level],
                    line_send_sems.at[t, d],
                    line_recv_sems.at[t, d],
                    line_peer(d),
                )
                for d in range(1, n_line)
            ]
        )
        line_all[t, level] = line_send[t]

    early = 5 * columns // 8
    for row in range(early):
        backward(row)
    start_line(0)
    for row in range(early, columns):
        backward(row)

    top = lax.broadcasted_iota(jnp.int32, (8, hidden), 0)
    ext_send[0:8, :] = jnp.where(
        top == channels + 1, totals[hidden : hidden + 8], totals_in[0:8] + totals_in[8:16]
    )
    ext_send[8:16, :] = totals_out[0:8]
    ext_plane_copies = [
        remote(
            ext_send,
            ext_plane_all.at[mine],
            ext_plane_send_sems.at[d],
            ext_plane_recv_sems.at[d],
            plane_peer(d)[1],
        )
        for d in range(1, n_plane)
    ]
    ext_plane_all[mine] = ext_send[...]
    for t in range(1, halves):
        start_line(t)

    ext_line_copies = []

    def start_ext_line():
        wait_all(ext_plane_copies)
        ext_line_send[...] = ordered_sum(ext_plane_all, n_plane)
        ext_line_copies.extend(
            remote(
                ext_line_send,
                ext_line_all.at[level],
                ext_line_send_sems.at[d],
                ext_line_recv_sems.at[d],
                line_peer(d),
            )
            for d in range(1, n_line)
        )
        ext_line_all[level] = ext_line_send[...]

    for copy in halo_copies:
        copy.wait()
    for c in range(channels):
        low_x[c, 0:z_elems, :] = x_halo[0, c]
        up_x[c, columns - z_elems : columns, :] = x_halo[1, c]
        if x_elems > 1:
            low_x[c, z_elems:columns, :] = adj_rows[c, 0 : columns - z_elems, :]
            up_x[c, 0 : columns - z_elems, :] = adj_rows[c, z_elems:columns, :]
        for i in range(x_elems):
            first, last = i * z_elems, (i + 1) * z_elems
            low_z[c, first : first + 1, :] = z_halo[0, c * x_elems + i]
            up_z[c, last - 1 : last, :] = z_halo[1, c * x_elems + i]
            if z_elems > 1:
                low_z[c, first + 1 : last, :] = adj_rows[c, first : last - 1, :]
                up_z[c, first : last - 1, :] = adj_rows[c, first + 1 : last, :]
    lane = lax.broadcasted_iota(jnp.int32, (columns, line), 1)
    row = lax.broadcasted_iota(jnp.int32, (columns, line), 0)
    spot_a, spot_b, spot_c, spot_j = (lane >> 4) & 3, (lane >> 2) & 3, lane & 3, lane >> 6
    bottom = jnp.zeros((columns, line), F32)
    ceiling = jnp.zeros((columns, line), F32)
    for i in range(x_elems):
        for k in range(z_elems):
            here = row == i * z_elems + k
            bottom = jnp.where(here, -2.0 * tags_ref[0, i, k].astype(F32), bottom)
            ceiling = jnp.where(here, -2.0 * tags_ref[1, i, k].astype(F32), ceiling)
    for c in range(channels):
        if c == channels // 2:
            start_ext_line()
        own = adj_rows[c]
        low_y = jnp.where(spot_j == 0, bottom * own, pltpu.roll(own, 52, 1) - own)
        up_y = jnp.where(
            spot_j == line // 64 - 1, ceiling * own, pltpu.roll(own, line - 52, 1) - own
        )
        jump = (
            jnp.where(spot_a == 0, pltpu.roll(low_x[c], line - 48, 1) - own, 0.0)
            + jnp.where(spot_a == 3, pltpu.roll(up_x[c], 48, 1) - own, 0.0)
            + jnp.where(spot_b == 0, low_y, 0.0)
            + jnp.where(spot_b == 3, up_y, 0.0)
            + jnp.where(spot_c == 0, pltpu.roll(low_z[c], line - 3, 1) - own, 0.0)
            + jnp.where(spot_c == 3, pltpu.roll(up_z[c], 3, 1) - own, 0.0)
        )
        back_rows[c] = own + 0.5 * KAPPA * jump + inv_norm * back_rows[c]
        for i in range(x_elems):
            gstate_ref[c, i] = back_rows[c, i * z_elems : (i + 1) * z_elems, :]
    stores = []

    def store(src, dst):
        copy = pltpu.make_async_copy(src, dst, store_sems.at[len(stores)])
        copy.start()
        stores.append(copy)

    store(gstate_ref, gstate_hbm)

    factor = 4.0 / math.sqrt(entry_count // channels)
    spread_copies = []
    for t in range(halves):
        wait_all(line_copies[t])
        result[t] = factor * ordered_sum(line_all.at[t], n_line)
        for d in range(1, n_plane):
            spread_copies.append(
                remote(
                    result.at[t],
                    gmid_hbm.at[block_of(mine, t)],
                    spread_send_sems.at[t, d],
                    spread_recv_sems.at[t, d],
                    plane_peer(d)[1],
                )
            )
        store(result.at[t], gmid_hbm.at[block_of(mine, t)])
    wait_all(ext_line_copies)
    small = factor * ordered_sum(ext_line_all, n_line)
    gin_ref[...] = small[0:channels]
    gbin_ref[...] = small[channels : channels + 1]
    gbmid_ref[...] = small[channels + 1 : channels + 2]
    gout_ref[...] = small[8 : 8 + channels]
    store(gin_ref, gin_hbm)
    store(gbin_ref, gbin_hbm)
    store(gbmid_ref, gbmid_hbm)
    store(gout_ref, gout_hbm)
    wait_all(spread_copies)
    wait_all(stores)


def writer(*refs):
    size = (len(refs) - 1) // 3
    sems = refs[-1]
    sources, results, held = refs[:size], refs[size : 2 * size], refs[2 * size : -1]
    loads = [
        pltpu.make_async_copy(sources[spot], held[spot], sems.at[spot]) for spot in range(size)
    ]
    stores = [
        pltpu.make_async_copy(held[spot], results[spot], sems.at[size + spot])
        for spot in range(size)
    ]
    for load in loads:
        load.start()
    for load, store in zip(loads, stores):
        load.wait()
        store.start()
    for store in stores:
        store.wait()


def per_device(dims, state, cotangent, local_inverse, wall_tags, w_in, b_in, w_mid, b_mid, w_out):
    gx, gz = dims
    channels, x_elems, z_elems, line = state.shape
    hidden = w_mid.shape[0]
    columns = x_elems * z_elems
    n_plane, n_line = gx * 4, gz // 4
    part = hidden // n_plane
    halves = 2 if part % 16 == 0 else 1
    span = part // halves
    vmem = pl.BlockSpec(memory_space=pltpu.VMEM)
    hbm = pl.BlockSpec(memory_space=pltpu.HBM)
    rows = pltpu.VMEM((channels, columns, line), F32)
    dma = pltpu.SemaphoreType.DMA

    def same(array):
        return pltpu.VMEM(array.shape, array.dtype)

    b_in, b_mid = b_in.reshape(1, hidden), b_mid.reshape(1, hidden)
    out_shape = (
        jax.ShapeDtypeStruct(state.shape, F32),
        jax.ShapeDtypeStruct((channels, hidden), F32),
        jax.ShapeDtypeStruct((1, hidden), F32),
        jax.ShapeDtypeStruct((hidden, hidden), F32),
        jax.ShapeDtypeStruct((1, hidden), F32),
        jax.ShapeDtypeStruct((channels, hidden), F32),
    )
    out = pl.pallas_call(
        functools.partial(kernel, dims),
        out_shape=out_shape,
        in_specs=[hbm] * 8 + [vmem],
        out_specs=(hbm,) * 6,
        scratch_shapes=[
            same(state),
            pltpu.VMEM((channels, hidden), F32),
            pltpu.VMEM((1, hidden), F32),
            pltpu.VMEM((1, hidden), F32),
            pltpu.VMEM((channels, hidden), F32),
            same(state),
            same(cotangent),
            same(local_inverse),
            pltpu.SMEM(wall_tags.shape, jnp.int32),
            same(w_in),
            same(b_in),
            same(w_mid),
            same(b_mid),
            pltpu.VMEM((columns, 8, line), F32),
            pltpu.VMEM((columns, 16, line), F32),
            rows,
            rows,
            rows,
            rows,
            rows,
            rows,
            pltpu.VMEM((2, channels, z_elems, line), F32),
            pltpu.VMEM((2, channels, z_elems, line), F32),
            pltpu.VMEM((2, channels * x_elems, 1, line), F32),
            pltpu.VMEM((2, channels * x_elems, 1, line), F32),
            pltpu.VMEM((hidden, 32), BF16),
            pltpu.VMEM((16, hidden), BF16),
            pltpu.VMEM((hidden, hidden), BF16),
            pltpu.VMEM((hidden, hidden), BF16),
            pltpu.VMEM((hidden, 16), BF16),
            pltpu.VMEM((hidden, 128), F32),
            pltpu.VMEM((columns, hidden + 32, line), BF16),
            pltpu.VMEM((columns, hidden, line), F32),
            pltpu.VMEM((columns, hidden, line), BF16),
            pltpu.VMEM((columns, hidden, line), BF16),
            pltpu.VMEM((hidden + 32, hidden), F32),
            pltpu.VMEM((32, hidden), F32),
            pltpu.VMEM((16, hidden), F32),
            pltpu.VMEM((1, 128), F32),
            pltpu.VMEM((gx * gz, 1, 128), F32),
            pltpu.VMEM((halves, n_plane, span, hidden), F32),
            pltpu.VMEM((halves, span, hidden), F32),
            pltpu.VMEM((halves, n_line, span, hidden), F32),
            pltpu.VMEM((halves, span, hidden), F32),
            pltpu.VMEM((16, hidden), F32),
            pltpu.VMEM((n_plane, 16, hidden), F32),
            pltpu.VMEM((16, hidden), F32),
            pltpu.VMEM((n_line, 16, hidden), F32),
            dma((11,)),
            dma((halves + 5,)),
            dma((2,)),
            dma((4,)),
            dma((4,)),
            dma((halves, n_plane)),
            dma((halves, n_plane)),
            dma((halves, n_line)),
            dma((halves, n_line)),
            dma((n_plane,)),
            dma((n_plane,)),
            dma((n_line,)),
            dma((n_line,)),
            dma((halves, n_plane)),
            dma((halves, n_plane)),
        ],
        compiler_params=pltpu.CompilerParams(
            collective_id=0, has_side_effects=True, vmem_limit_bytes=62 * 1024 * 1024
        ),
    )(state, cotangent, local_inverse, wall_tags, w_in, b_in, w_mid, b_mid, w_out.T)
    out = pl.pallas_call(
        writer,
        out_shape=out_shape,
        in_specs=[hbm] * 6,
        out_specs=(hbm,) * 6,
        scratch_shapes=[pltpu.VMEM(o.shape, F32) for o in out_shape] + [dma((12,))],
        compiler_params=pltpu.CompilerParams(vmem_limit_bytes=62 * 1024 * 1024),
    )(*out)
    return out[0], out[1], out[2].reshape(hidden), out[3], out[4].reshape(hidden), out[5].T


def solution(mesh):
    placed = (
        P(None, "gx", "gz", None),
        P(None, "gx", "gz", None),
        P(None, "gx", "gz", None),
        P(None, "gx", "gz"),
        P(),
        P(),
        P(),
        P(),
        P(),
    )
    return jax.shard_map(
        functools.partial(per_device, (mesh.shape["gx"], mesh.shape["gz"])),
        mesh=mesh,
        in_specs=placed,
        out_specs=(P(None, "gx", "gz", None), P(), P(), P(), P(), P()),
        check_vma=False,
    )
```

```python
import functools
import math

import jax
import jax.numpy as jnp
from jax import lax
from jax.experimental import pallas as pl
from jax.experimental.pallas import tpu as pltpu
from jax.sharding import PartitionSpec as P

KAPPA = 0.5
DT_STEP = 0.5
EPS = 1e-06
F32 = jnp.float32
BF16 = jnp.bfloat16
MESH = pl.DeviceIdType.MESH


def nt_dot(first_op, second_op):
    return lax.dot_general(
        first_op, second_op, (((1,), (1,)), ((), ())), preferred_element_type=F32
    )


def nn_dot(first_op, second_op):
    return jnp.dot(first_op, second_op, preferred_element_type=F32)


def rounded(value):
    return value.astype(BF16).astype(F32)


def kernel(
    dims,
    state_hbm,
    cot_hbm,
    inv_hbm,
    tags_hbm,
    w_in_hbm,
    b_in_hbm,
    w_mid_hbm,
    b_mid_hbm,
    w_out_ref,
    gstate_ref,
    gin_ref,
    gbin_ref,
    gmid_ref,
    gbmid_ref,
    gout_ref,
    state_ref,
    cot_ref,
    inv_ref,
    tags_ref,
    w_in_ref,
    b_in_ref,
    w_mid_ref,
    b_mid_ref,
    state_rows,
    grad_rows,
    adj_rows,
    back_rows,
    low_x,
    up_x,
    low_z,
    up_z,
    x_send,
    x_halo,
    z_send,
    z_halo,
    w_first,
    w_back,
    w_mid_t,
    w_mid_half,
    w_out_half,
    bias_mid,
    joints,
    bends,
    hiddens,
    deltas,
    totals,
    totals_in,
    totals_out,
    norm_mine,
    norm_all,
    plane_all,
    line_send,
    line_all,
    result,
    ext_send,
    ext_plane_all,
    ext_line_send,
    ext_line_all,
    load_sems,
    norm_sems,
    halo_send_sems,
    halo_recv_sems,
    plane_send_sems,
    plane_recv_sems,
    line_send_sems,
    line_recv_sems,
    ext_plane_send_sems,
    ext_plane_recv_sems,
    ext_line_send_sems,
    ext_line_recv_sems,
    spread_send_sems,
    spread_recv_sems,
):
    gx, gz = dims
    channels, x_elems, z_elems, line = state_ref.shape
    hidden = w_mid_ref.shape[0]
    columns = x_elems * z_elems
    count = gx * gz
    n_plane, n_line = gx * 4, gz // 4
    part = hidden // n_plane
    halves, _, span, _ = plane_all.shape
    nodes = inv_ref.shape[0]
    pieces = 4
    piece = nodes // pieces
    my_x, my_z = lax.axis_index("gx"), lax.axis_index("gz")
    me = my_x * gz + my_z
    spot_z, level = my_z % 4, my_z // 4
    mine = my_x * 4 + spot_z

    loads = [
        pltpu.make_async_copy(src, dst, load_sems.at[spot])
        for spot, (src, dst) in enumerate(
            (
                (state_hbm, state_ref),
                (cot_hbm, cot_ref),
                (w_in_hbm, w_in_ref),
                (b_in_hbm, b_in_ref),
                (w_mid_hbm, w_mid_ref),
                (b_mid_hbm, b_mid_ref),
                (tags_hbm, tags_ref),
            )
        )
    ]
    inv_loads = [
        pltpu.make_async_copy(
            inv_hbm.at[pl.ds(p * piece, piece)],
            inv_ref.at[pl.ds(p * piece, piece)],
            load_sems.at[len(loads) + p],
        )
        for p in range(pieces)
    ]
    for load in loads[2:] + loads[:2] + inv_loads:
        load.start()

    barrier = pltpu.get_barrier_semaphore()

    def greet(step, carry):
        to = lax.rem(me + step, count)
        pl.semaphore_signal(
            barrier, inc=1, device_id=(to // gz, lax.rem(to, gz)), device_id_type=MESH
        )
        return carry

    lax.fori_loop(1, count, greet, 0)

    loads[0].wait()
    squares = state_ref[...] * state_ref[...]
    squares = jnp.sum(jnp.sum(squares, axis=0), axis=0)
    folded = squares[:, :128]
    for start in range(128, line, 128):
        folded = folded + squares[:, start : start + 128]
    norm_mine[...] = jnp.sum(folded, axis=0, keepdims=True)

    pl.semaphore_wait(barrier, count - 1)

    def send_norm(step, carry):
        to = lax.rem(me + step, count)
        pltpu.make_async_remote_copy(
            src_ref=norm_mine,
            dst_ref=norm_all.at[step - 1],
            send_sem=norm_sems.at[0],
            recv_sem=norm_sems.at[1],
            device_id=(to // gz, lax.rem(to, gz)),
            device_id_type=MESH,
        ).start()
        return carry

    lax.fori_loop(1, count, send_norm, 0)

    for load in loads[2:]:
        load.wait()
    w_in = w_in_ref[...]
    w_high = rounded(w_in)
    w_low = rounded(w_in - w_high)
    b_in = b_in_ref[...]
    b_high = rounded(b_in)
    b_next = rounded(b_in - b_high)
    b_last = rounded(b_in - b_high - b_next)
    joint_rows = jnp.concatenate(
        [w_high, b_high, b_next, b_last, w_high, jnp.zeros((8 - channels, hidden), F32)]
        + [w_low, jnp.zeros((16 - channels, hidden), F32)],
        axis=0,
    )
    w_first[...] = (0.5 * joint_rows).T.astype(BF16)
    w_back[...] = joint_rows[8:24].astype(BF16)
    w_mid = 0.5 * w_mid_ref[...].astype(F32)
    w_mid_half[...] = w_mid.astype(BF16)
    w_mid_t[...] = w_mid.T.astype(BF16)
    w_out_half[...] = jnp.concatenate(
        [0.5 * w_out_ref[...].astype(F32), jnp.zeros((16 - channels, hidden), F32)], axis=0
    ).T.astype(BF16)
    bias = jnp.broadcast_to(0.5 * b_mid_ref[...], (128, hidden)).T
    bias_mid[...] = bias
    totals[...] = jnp.zeros_like(totals)
    totals_in[...] = jnp.zeros_like(totals_in)
    totals_out[...] = jnp.zeros_like(totals_out)

    loads[1].wait()
    for c in range(channels):
        for i in range(x_elems):
            low_x[c, i * z_elems : (i + 1) * z_elems, :] = cot_ref[c, i]
    lane = lax.broadcasted_iota(jnp.int32, (columns, 128), 1)
    first_lane = lane & 64
    blocks = line // 128

    def adjoint_step(n, sums):
        spot = first_lane + n
        rows = jnp.concatenate([inv_ref[n, i] for i in range(x_elems)], axis=0)
        out = []
        for c in range(channels):
            for t in range(blocks):
                tile = low_x[c, :, t * 128 : (t + 1) * 128]
                spread = jnp.take_along_axis(tile, spot, axis=1)
                out.append(
                    sums[c * blocks + t] + rows[:, t * 128 : (t + 1) * 128] * spread
                )
        return tuple(out)

    sums = (jnp.zeros((columns, 128), F32),) * (channels * blocks)
    for p in range(pieces):
        inv_loads[p].wait()
        sums = lax.fori_loop(p * piece, (p + 1) * piece, adjoint_step, sums, unroll=piece)
    for c in range(channels):
        for t in range(blocks):
            adj_rows[c, :, t * 128 : (t + 1) * 128] = sums[c * blocks + t]

    for c in range(channels):
        x_send[0, c] = adj_rows[c, 0:z_elems, :]
        x_send[1, c] = adj_rows[c, columns - z_elems : columns, :]
        for i in range(x_elems):
            z_send[0, c * x_elems + i] = adj_rows[c, i * z_elems : i * z_elems + 1, :]
            z_send[1, c * x_elems + i] = adj_rows[
                c, (i + 1) * z_elems - 1 : (i + 1) * z_elems, :
            ]
    halo_copies = []
    for spot, (src, dst, to) in enumerate(
        (
            (x_send.at[0], x_halo.at[1], (lax.rem(my_x + gx - 1, gx), my_z)),
            (x_send.at[1], x_halo.at[0], (lax.rem(my_x + 1, gx), my_z)),
            (z_send.at[0], z_halo.at[1], (my_x, lax.rem(my_z + gz - 1, gz))),
            (z_send.at[1], z_halo.at[0], (my_x, lax.rem(my_z + 1, gz))),
        )
    ):
        copy = pltpu.make_async_remote_copy(
            src_ref=src,
            dst_ref=dst,
            send_sem=halo_send_sems.at[spot],
            recv_sem=halo_recv_sems.at[spot],
            device_id=to,
            device_id_type=MESH,
        )
        copy.start()
        halo_copies.append(copy)

    for i in range(x_elems):
        for k in range(z_elems):
            row = i * z_elems + k
            state_rows[row] = jnp.ones((8, line), F32)
            grad_rows[row] = jnp.zeros((16, line), F32)
            for c in range(channels):
                state_rows[row, c : c + 1, :] = state_ref[c, i, k : k + 1, :]
                grad_rows[row, c : c + 1, :] = DT_STEP * adj_rows[c, row : row + 1, :]
    whole = norm_all.at[pl.ds(0, count - 1)]
    pltpu.make_async_copy(whole, whole, norm_sems.at[0]).wait()
    pltpu.make_async_copy(whole, whole, norm_sems.at[1]).wait()
    sum_squares = norm_mine[...] + jnp.sum(norm_all[0 : count - 1], axis=0)
    sum_squares = jnp.sum(sum_squares, axis=1, keepdims=True)
    entry_count = channels * columns * line * count
    inv_norm = lax.rsqrt(sum_squares / entry_count + EPS)
    row_index = lax.broadcasted_iota(jnp.int32, (8, line), 0)
    scale = jnp.where(row_index < channels, jnp.broadcast_to(inv_norm, (8, line)), 1.0)

    def first_layer(row):
        scaled = state_rows[row] * scale
        high = rounded(scaled)
        low = scaled - high
        inputs = jnp.concatenate([high, low, high, jnp.zeros_like(high)], axis=0).astype(BF16)
        joints[row, hidden:, :] = inputs
        pre = nn_dot(w_first[...], inputs)
        bend = jnp.tanh(pre)
        gate = 1.0 + bend
        act = pre * gate
        bends[row] = bend
        joints[row, :hidden, :] = act.astype(BF16)

    def second_layer(row):
        pre = nn_dot(w_mid_t[...], joints[row, :hidden, :])
        pre = pre + jnp.concatenate([bias_mid[...]] * (line // 128), axis=1)
        bend = jnp.tanh(pre)
        gate = 1.0 + bend
        act = pre * gate
        slope_two = gate + act * (1.0 - bend)
        out_grad = grad_rows[row].astype(BF16)
        hiddens[row] = act.astype(BF16)
        back_two = nn_dot(w_out_half[...], out_grad)
        deltas[row] = (back_two * slope_two).astype(BF16)

    def last_layer(row):
        totals[...] += nt_dot(joints[row], deltas[row])

    for step in range(columns + 2):
        if step < columns:
            first_layer(step)
        if 1 <= step <= columns:
            second_layer(step - 1)
        if step >= 2:
            last_layer(step - 2)

    def backward(row):
        bend = bends[row]
        slope = 1.0 + bend + joints[row, :hidden, :].astype(F32) * (1.0 - bend)
        delta_one = nn_dot(w_mid_half[...], deltas[row]) * slope
        delta_one = delta_one.astype(BF16)
        totals_in[...] += nt_dot(joints[row, hidden:, :], delta_one)
        totals_out[...] += nt_dot(grad_rows[row].astype(BF16), hiddens[row])
        back = nn_dot(w_back[...], delta_one)
        back = back[:8] + back[8:]
        for c in range(channels):
            back_rows[c, row : row + 1, :] = back[c : c + 1, :]

    def remote(src, dst, send_sem, recv_sem, to):
        copy = pltpu.make_async_remote_copy(
            src_ref=src,
            dst_ref=dst,
            send_sem=send_sem,
            recv_sem=recv_sem,
            device_id=to,
            device_id_type=MESH,
        )
        copy.start()
        return copy

    def plane_peer(d):
        to = lax.rem(mine + d, n_plane)
        return to, (to // 4, level * 4 + lax.rem(to, 4))

    def line_peer(d):
        return (my_x, lax.rem(level + d, n_line) * 4 + spot_z)

    def ordered_sum(ref, size):
        return sum((ref[q] for q in range(1, size)), ref[0])

    def wait_all(copies):
        for copy in copies:
            copy.wait()

    def block_of(owner, t):
        return pl.ds(pl.multiple_of(owner * part + t * span, span), span)

    plane_copies = []
    for t in range(halves):
        copies = []
        for d in range(1, n_plane):
            to, device = plane_peer(d)
            copies.append(
                remote(
                    totals.at[block_of(to, t)],
                    plane_all.at[t, mine],
                    plane_send_sems.at[t, d],
                    plane_recv_sems.at[t, d],
                    device,
                )
            )
        plane_copies.append(copies)
        plane_all[t, mine] = totals[block_of(mine, t), :]

    line_copies = []

    def start_line(t):
        wait_all(plane_copies[t])
        line_send[t] = ordered_sum(plane_all.at[t], n_plane)
        line_copies.append(
            [
                remote(
                    line_send.at[t],
                    line_all.at[t, level],
                    line_send_sems.at[t, d],
                    line_recv_sems.at[t, d],
                    line_peer(d),
                )
                for d in range(1, n_line)
            ]
        )
        line_all[t, level] = line_send[t]

    early = 5 * columns // 8
    for row in range(early):
        backward(row)
    start_line(0)
    for row in range(early, columns):
        backward(row)

    top = lax.broadcasted_iota(jnp.int32, (8, hidden), 0)
    ext_send[0:8, :] = jnp.where(
        top == channels + 1, totals[hidden : hidden + 8], totals_in[0:8] + totals_in[8:16]
    )
    ext_send[8:16, :] = totals_out[0:8]
    ext_plane_copies = [
        remote(
            ext_send,
            ext_plane_all.at[mine],
            ext_plane_send_sems.at[d],
            ext_plane_recv_sems.at[d],
            plane_peer(d)[1],
        )
        for d in range(1, n_plane)
    ]
    ext_plane_all[mine] = ext_send[...]
    for t in range(1, halves):
        start_line(t)

    ext_line_copies = []

    def start_ext_line():
        wait_all(ext_plane_copies)
        ext_line_send[...] = ordered_sum(ext_plane_all, n_plane)
        ext_line_copies.extend(
            remote(
                ext_line_send,
                ext_line_all.at[level],
                ext_line_send_sems.at[d],
                ext_line_recv_sems.at[d],
                line_peer(d),
            )
            for d in range(1, n_line)
        )
        ext_line_all[level] = ext_line_send[...]

    for copy in halo_copies:
        copy.wait()
    for c in range(channels):
        low_x[c, 0:z_elems, :] = x_halo[0, c]
        up_x[c, columns - z_elems : columns, :] = x_halo[1, c]
        if x_elems > 1:
            low_x[c, z_elems:columns, :] = adj_rows[c, 0 : columns - z_elems, :]
            up_x[c, 0 : columns - z_elems, :] = adj_rows[c, z_elems:columns, :]
        for i in range(x_elems):
            first, last = i * z_elems, (i + 1) * z_elems
            low_z[c, first : first + 1, :] = z_halo[0, c * x_elems + i]
            up_z[c, last - 1 : last, :] = z_halo[1, c * x_elems + i]
            if z_elems > 1:
                low_z[c, first + 1 : last, :] = adj_rows[c, first : last - 1, :]
                up_z[c, first : last - 1, :] = adj_rows[c, first + 1 : last, :]
    lane = lax.broadcasted_iota(jnp.int32, (columns, line), 1)
    row = lax.broadcasted_iota(jnp.int32, (columns, line), 0)
    spot_a, spot_b, spot_c, spot_j = (lane >> 4) & 3, (lane >> 2) & 3, lane & 3, lane >> 6
    bottom = jnp.zeros((columns, line), F32)
    ceiling = jnp.zeros((columns, line), F32)
    for i in range(x_elems):
        for k in range(z_elems):
            here = row == i * z_elems + k
            bottom = jnp.where(here, -2.0 * tags_ref[0, i, k].astype(F32), bottom)
            ceiling = jnp.where(here, -2.0 * tags_ref[1, i, k].astype(F32), ceiling)
    for c in range(channels):
        if c == channels // 2:
            start_ext_line()
        own = adj_rows[c]
        low_y = jnp.where(spot_j == 0, bottom * own, pltpu.roll(own, 52, 1) - own)
        up_y = jnp.where(
            spot_j == line // 64 - 1, ceiling * own, pltpu.roll(own, line - 52, 1) - own
        )
        jump = (
            jnp.where(spot_a == 0, pltpu.roll(low_x[c], line - 48, 1) - own, 0.0)
            + jnp.where(spot_a == 3, pltpu.roll(up_x[c], 48, 1) - own, 0.0)
            + jnp.where(spot_b == 0, low_y, 0.0)
            + jnp.where(spot_b == 3, up_y, 0.0)
            + jnp.where(spot_c == 0, pltpu.roll(low_z[c], line - 3, 1) - own, 0.0)
            + jnp.where(spot_c == 3, pltpu.roll(up_z[c], 3, 1) - own, 0.0)
        )
        back_rows[c] = own + 0.5 * KAPPA * jump + inv_norm * back_rows[c]
        for i in range(x_elems):
            gstate_ref[c, i] = back_rows[c, i * z_elems : (i + 1) * z_elems, :]
    factor = 4.0 / math.sqrt(entry_count // channels)
    spread_copies = []
    for t in range(halves):
        wait_all(line_copies[t])
        result[t] = factor * ordered_sum(line_all.at[t], n_line)
        for d in range(1, n_plane):
            spread_copies.append(
                remote(
                    result.at[t],
                    gmid_ref.at[block_of(mine, t)],
                    spread_send_sems.at[t, d],
                    spread_recv_sems.at[t, d],
                    plane_peer(d)[1],
                )
            )
        gmid_ref[block_of(mine, t), :] = result[t]
    wait_all(ext_line_copies)
    small = factor * ordered_sum(ext_line_all, n_line)
    gin_ref[...] = small[0:channels]
    gbin_ref[...] = small[channels : channels + 1]
    gbmid_ref[...] = small[channels + 1 : channels + 2]
    gout_ref[...] = small[8 : 8 + channels]
    wait_all(spread_copies)


def writer(*refs):
    size = len(refs) // 2
    copies = [
        pltpu.make_async_copy(refs[spot], refs[size + spot], refs[-1].at[spot])
        for spot in range(size)
    ]
    for copy in copies:
        copy.start()
    for copy in copies:
        copy.wait()


def per_device(dims, state, cotangent, local_inverse, wall_tags, w_in, b_in, w_mid, b_mid, w_out):
    gx, gz = dims
    channels, x_elems, z_elems, line = state.shape
    hidden = w_mid.shape[0]
    columns = x_elems * z_elems
    n_plane, n_line = gx * 4, gz // 4
    part = hidden // n_plane
    halves = 2 if part % 16 == 0 else 1
    span = part // halves
    vmem = pl.BlockSpec(memory_space=pltpu.VMEM)
    hbm = pl.BlockSpec(memory_space=pltpu.HBM)
    rows = pltpu.VMEM((channels, columns, line), F32)
    dma = pltpu.SemaphoreType.DMA

    def same(array):
        return pltpu.VMEM(array.shape, array.dtype)

    b_in, b_mid = b_in.reshape(1, hidden), b_mid.reshape(1, hidden)
    out_shape = (
        jax.ShapeDtypeStruct(state.shape, F32),
        jax.ShapeDtypeStruct((channels, hidden), F32),
        jax.ShapeDtypeStruct((1, hidden), F32),
        jax.ShapeDtypeStruct((hidden, hidden), F32),
        jax.ShapeDtypeStruct((1, hidden), F32),
        jax.ShapeDtypeStruct((channels, hidden), F32),
    )
    out = pl.pallas_call(
        functools.partial(kernel, dims),
        out_shape=tuple(pltpu.VMEM(o.shape, F32) for o in out_shape),
        in_specs=[hbm] * 8 + [vmem],
        out_specs=(vmem,) * 6,
        scratch_shapes=[
            same(state),
            same(cotangent),
            same(local_inverse),
            pltpu.SMEM(wall_tags.shape, jnp.int32),
            same(w_in),
            same(b_in),
            same(w_mid),
            same(b_mid),
            pltpu.VMEM((columns, 8, line), F32),
            pltpu.VMEM((columns, 16, line), F32),
            rows,
            rows,
            rows,
            rows,
            rows,
            rows,
            pltpu.VMEM((2, channels, z_elems, line), F32),
            pltpu.VMEM((2, channels, z_elems, line), F32),
            pltpu.VMEM((2, channels * x_elems, 1, line), F32),
            pltpu.VMEM((2, channels * x_elems, 1, line), F32),
            pltpu.VMEM((hidden, 32), BF16),
            pltpu.VMEM((16, hidden), BF16),
            pltpu.VMEM((hidden, hidden), BF16),
            pltpu.VMEM((hidden, hidden), BF16),
            pltpu.VMEM((hidden, 16), BF16),
            pltpu.VMEM((hidden, 128), F32),
            pltpu.VMEM((columns, hidden + 32, line), BF16),
            pltpu.VMEM((columns, hidden, line), F32),
            pltpu.VMEM((columns, hidden, line), BF16),
            pltpu.VMEM((columns, hidden, line), BF16),
            pltpu.VMEM((hidden + 32, hidden), F32),
            pltpu.VMEM((32, hidden), F32),
            pltpu.VMEM((16, hidden), F32),
            pltpu.VMEM((1, 128), F32),
            pltpu.VMEM((gx * gz, 1, 128), F32),
            pltpu.VMEM((halves, n_plane, span, hidden), F32),
            pltpu.VMEM((halves, span, hidden), F32),
            pltpu.VMEM((halves, n_line, span, hidden), F32),
            pltpu.VMEM((halves, span, hidden), F32),
            pltpu.VMEM((16, hidden), F32),
            pltpu.VMEM((n_plane, 16, hidden), F32),
            pltpu.VMEM((16, hidden), F32),
            pltpu.VMEM((n_line, 16, hidden), F32),
            dma((11,)),
            dma((2,)),
            dma((4,)),
            dma((4,)),
            dma((halves, n_plane)),
            dma((halves, n_plane)),
            dma((halves, n_line)),
            dma((halves, n_line)),
            dma((n_plane,)),
            dma((n_plane,)),
            dma((n_line,)),
            dma((n_line,)),
            dma((halves, n_plane)),
            dma((halves, n_plane)),
        ],
        compiler_params=pltpu.CompilerParams(
            collective_id=0, has_side_effects=True, vmem_limit_bytes=62 * 1024 * 1024
        ),
    )(state, cotangent, local_inverse, wall_tags, w_in, b_in, w_mid, b_mid, w_out.T)
    out = pl.pallas_call(
        writer,
        out_shape=tuple(pltpu.HBM(o.shape, F32) for o in out_shape),
        in_specs=[vmem] * 6,
        out_specs=(hbm,) * 6,
        scratch_shapes=[dma((6,))],
        compiler_params=pltpu.CompilerParams(vmem_limit_bytes=8 * 1024 * 1024),
    )(*out)
    return out[0], out[1], out[2].reshape(hidden), out[3], out[4].reshape(hidden), out[5].T


def solution(mesh):
    placed = (
        P(None, "gx", "gz", None),
        P(None, "gx", "gz", None),
        P(None, "gx", "gz", None),
        P(None, "gx", "gz"),
        P(),
        P(),
        P(),
        P(),
        P(),
    )
    return jax.shard_map(
        functools.partial(per_device, (mesh.shape["gx"], mesh.shape["gz"])),
        mesh=mesh,
        in_specs=placed,
        out_specs=(P(None, "gx", "gz", None), P(), P(), P(), P(), P()),
        check_vma=False,
    )
```
